32 devices in a mesh: parts: 2 (over y), tmpl: 4 (over z), sta: 2 (over x), sub: 2 (over core).
Axes of the slice: x: 2, y: 2, z: 4, core: 2. Of those that a mesh axis runs over, the one named last changes fastest.
Arguments:
- traces: bfloat16 [16, 3, 1536], P(('tmpl', 'sta'), None, ('parts', 'sub')), parts along dimension 2
- trace_tail: bfloat16 [16, 3, 726], P(('tmpl', 'sta'), None, 'parts'), parts along dimension 2
- templates: bfloat16 [32, 3, 300], P('tmpl')
- win_lengths: int32 [32], replicated, may hold values from 150 to 300
- moveouts: int32 [32, 16], replicated, may hold values from 0 to 63
- chan_mask: int32 [32, 3], P('parts'), parts along dimension 0, may hold values 0 or 1
- subnet: int32 [16], replicated, may hold values from 0 to 1
Outputs:
- network_stack: float32 [32, 2, 1536], P(('tmpl', 'sta'), None, ('parts', 'sub')), parts along dimension 2
The draws below stay inside these ranges and needn't reach their ends.
There are 2 independent parts, one for each index of `parts`. The reference program is written for one: setup_inputs(seed, part) draws one part's arguments, and reference() takes and returns one part's arrays. A program takes and returns all parts, laid end to end along the dimension named above; an argument that names none is the same for every part. Nothing has to cross between parts.
All inputs are finite; a program needn't handle non-finite values.
Results may differ from the reference program's by a relative error of at most 0.0003.
Values may be sent and summed in bfloat16 or wider, within the bound.
A program may use at most 64 MiB of HBM per device.

```python
import math
import jax
import jax.numpy as jnp
from jax import lax

TLEN = 300
MOVE = 64
REGIONS = 2
K_DEV = 8
HALO = 363
STATIONS = 16
TEMPLATES = 32
NT = 768


def rough_wave(key, dims_out, lowest, highest, block_len):
    noise_key, scale_key, env_key = jax.random.split(key, 3)
    noise_part = jnp.clip(jax.random.normal(noise_key, dims_out, jnp.float32), -6.0, 6.0)
    upper = highest
    scales = jnp.exp(jax.random.uniform(scale_key, dims_out[:2] + (1,), jnp.float32, math.log(lowest), math.log(upper)))
    block_count = -(-dims_out[2] // block_len)
    envelope = jnp.exp(jax.random.uniform(env_key, dims_out[:2] + (block_count,), jnp.float32, math.log(0.3), math.log(3.0)))
    envelope = jnp.repeat(envelope, block_len, axis=2)[:, :, :dims_out[2]]
    return (noise_part * scales * envelope).astype(jnp.bfloat16)


def draw_traces(key, part):
    return rough_wave(key, (STATIONS, 3, NT), 1.0, 10.0, 32)


def draw_trace_tail(key, part):
    return rough_wave(key, (STATIONS, 3, HALO), 1.0, 10.0, 32)


def draw_templates(key, part):
    return rough_wave(key, (TEMPLATES, 3, TLEN), 0.1, 1.0, 25)


def with_ends(result, key, smallest, high):
    index_at = [jax.random.randint(jax.random.fold_in(key, axis), (), 0, length) for axis, length in enumerate(result.shape)]
    main_axis = result.shape.index(max(result.shape))
    beside = index_at[:main_axis] + [(index_at[main_axis] + 1) % result.shape[main_axis]] + index_at[main_axis + 1:]
    return result.at[tuple(index_at)].set(smallest).at[tuple(beside)].set(high)


def setup_inputs(seed: int = 0, part: int = 0) -> dict:
    splits = jax.random.split(jax.random.key(seed), 8)
    part_keys = jax.random.split(jax.random.fold_in(splits[7], part), 8)
    traces = draw_traces(jax.random.fold_in(jax.random.fold_in(splits[7], part), 71), part)
    trace_tail = draw_trace_tail(jax.random.fold_in(jax.random.fold_in(splits[7], part), 71), part)
    templates = draw_templates(jax.random.fold_in(splits[7], 71), part)
    win_lengths = with_ends(jax.random.randint(splits[3], (TEMPLATES,), TLEN // 2, TLEN + 1), jax.random.fold_in(splits[3], 1), TLEN // 2, TLEN).astype(jnp.int32)
    moveouts = with_ends(jax.random.randint(splits[4], (TEMPLATES, STATIONS), 0, MOVE), jax.random.fold_in(splits[4], 1), 0, MOVE - 1).astype(jnp.int32)
    chan_mask = with_ends((jax.random.randint(part_keys[5], (STATIONS, 3), 0, 4) < 3).astype(jnp.int32), jax.random.fold_in(part_keys[5], 1), 0, 1)
    subnet = with_ends(jax.random.randint(splits[6], (STATIONS,), 0, REGIONS), jax.random.fold_in(splits[6], 1), 0, REGIONS - 1).astype(jnp.int32)
    return {"traces": traces, "trace_tail": trace_tail, "templates": templates, "win_lengths": win_lengths, "moveouts": moveouts, "chan_mask": chan_mask, "subnet": subnet}


def correlate(extended, tmpl_rows, win_rows, mask_rows, lag_rows, subnet_rows, t_out):
    span_len = tmpl_rows.shape[2]
    t_corr = extended.shape[2] - span_len + 1
    live_count = jnp.maximum(lax.optimization_barrier(jnp.sum(mask_rows, axis=1)), 1).astype(jnp.float32)
    weights = mask_rows.astype(jnp.float32)
    win_float = win_rows.astype(jnp.float32)
    running = jnp.zeros((extended.shape[0], tmpl_rows.shape[0], t_corr), jnp.float32)
    for channel in range(3):
        signal = extended[:, channel:channel + 1, :]
        corr = lax.conv_general_dilated(signal, tmpl_rows[:, channel:channel + 1, :], (1,), 'VALID', dimension_numbers=('NCH', 'OIH', 'NCH'), preferred_element_type=jnp.float32)
        squares = jnp.square(extended[:, channel, :].astype(jnp.float32))
        prefix = jnp.concatenate([jnp.zeros((squares.shape[0], 1), jnp.float32), jnp.cumsum(squares, axis=1)], axis=1)

        def window_sum(width):
            return lax.dynamic_slice_in_dim(prefix, width, t_corr, 1) - prefix[:, :t_corr]
        energy = jax.vmap(window_sum, out_axes=1)(win_rows.astype(jnp.int32))
        tmpl_norm = jnp.sqrt(lax.optimization_barrier(jnp.sum(jnp.square(tmpl_rows[:, channel, :].astype(jnp.float32)), axis=1)) + 1e-06)
        denom = tmpl_norm[None, :, None] * jnp.sqrt(energy + 1e-05 * win_float[None, :, None])
        running = running + weights[:, channel][:, None, None] * corr / denom
    coherent = running / live_count[:, None, None]

    def align(series_rows, shift_rows):
        return jax.vmap(lambda series, lag_value: lax.dynamic_slice_in_dim(series, lag_value, t_out, 0))(series_rows, shift_rows)
    aligned = jax.vmap(align)(coherent, jnp.transpose(lag_rows).astype(jnp.int32))
    member = (subnet_rows[:, None] == jnp.arange(REGIONS)[None, :]).astype(jnp.float32)
    return jnp.einsum('skt,sr->krt', aligned, member, precision=lax.Precision.HIGHEST)

def reference(traces, trace_tail, templates, win_lengths, moveouts, chan_mask, subnet):
    extended = jnp.concatenate([traces, trace_tail], axis=2)
    t_total = traces.shape[2]
    n_blocks = TEMPLATES // K_DEV
    tmpl_blocks = templates.reshape(n_blocks, K_DEV, 3, TLEN)
    win_blocks = win_lengths.reshape(n_blocks, K_DEV)
    lag_blocks = moveouts.reshape(n_blocks, K_DEV, STATIONS)

    def one_block(packed):
        return correlate(extended, packed[0], packed[1], chan_mask, packed[2], subnet, t_total)
    stacked = lax.map(one_block, (tmpl_blocks, win_blocks, lag_blocks))
    return stacked.reshape(TEMPLATES, REGIONS, t_total)
```

```python
import functools

import jax
import jax.numpy as jnp
from jax import lax
from jax.experimental import pallas as pl
from jax.experimental.pallas import tpu as pltpu
from jax.sharding import PartitionSpec as P

REGIONS = 2
CHANNELS = 3
LANES = 128
GROUP = 16
PITCH = 4
F32 = jnp.float32
BF16 = jnp.bfloat16
NT_DIMS = (((1,), (1,)), ((), ()))


def ceil_div(a, b):
    return -(-a // b)


def each(count, body):
    if count <= 16:
        for i in range(count):
            body(i)
    else:
        lax.fori_loop(0, count, lambda i, c: (body(i), c)[1], 0)


def kernel(
    n_sta, n_own, share,
    traces, tail, templates, wins, lags, mask, subnet,
    out,
    stage, send, recv, ebuf, tpad, wt, bt, acc, send_sem, recv_sem,
):
    st_dev, _, t_dev = traces.shape
    halo = tail.shape[2]
    span = templates.shape[2]
    lag_bits = (halo - span).bit_length()
    own_blocks = t_dev // LANES
    u_blocks = ceil_div(t_dev + halo - span + 1, LANES)
    k_blocks = ceil_div(LANES + span - 1, LANES)
    width = k_blocks * LANES
    owners = GROUP // st_dev
    n_groups = n_own // owners
    everyone = 2 * n_own

    t_me = lax.axis_index("tmpl")
    a_me = lax.axis_index("sta")
    u_me = lax.axis_index("sub")
    own = t_me * n_sta + a_me
    flat = own * 2 + u_me

    def place(d):
        other = lax.rem(flat + d, everyone)
        return {"tmpl": other // (2 * n_sta), "sta": (other // 2) % n_sta, "sub": other % 2}

    barrier = pltpu.get_barrier_semaphore()

    def greet(i):
        pl.semaphore_signal(barrier, inc=1, device_id=place(i + 1), device_id_type=pl.DeviceIdType.MESH)

    each(everyone - 1, greet)

    stage[...] = jnp.zeros_like(stage)
    for s in range(st_dev):
        rows = pl.ds(s * PITCH, CHANNELS)
        stage[0, rows, :] = traces[s].astype(F32)
        stage[1, rows, pl.ds(0, halo)] = tail[s].astype(F32)
    main = stage[0]
    rim = jnp.where(u_me == 1, main, stage[1])
    send[0] = main.astype(BF16)
    send[1] = rim.astype(BF16)
    recv[own, 0] = main.astype(BF16)

    pl.semaphore_wait(barrier, everyone - 1)

    def outgoing(i):
        d = i + 1
        half = d % 2
        return pltpu.make_async_remote_copy(
            src_ref=send.at[half],
            dst_ref=recv.at[own, half],
            send_sem=send_sem.at[i],
            recv_sem=recv_sem.at[i],
            device_id=place(d),
            device_id_type=pl.DeviceIdType.MESH,
        )

    each(everyone - 1, lambda i: outgoing(i).start())

    tpad[...] = jnp.zeros_like(tpad)
    for k in range(share):
        tpad[k, pl.ds(0, CHANNELS), pl.ds(0, span)] = templates[a_me * share + k].astype(F32)
    row_at = lax.broadcasted_iota(jnp.int32, (LANES, width), 0)
    col_at = lax.broadcasted_iota(jnp.int32, (LANES, width), 1)
    apart = col_at - row_at
    first = own * share
    inv_norm = []
    floor_rows = []
    for k in range(share):
        taps = tpad[k]
        power = jnp.sum(taps * taps, axis=1, keepdims=True)
        inv_norm.append(1.0 / jnp.sqrt(power + 1e-06))
        win = wins[first + k]
        floor_rows.append(jnp.full((1, LANES), 1e-05 * win.astype(F32), F32))
        band = jnp.logical_and(apart >= 0, apart < win)
        bt[pl.ds(k * LANES, LANES), :] = jnp.where(band, 1.0, 0.0).astype(BF16)
        for c in range(CHANNELS):
            line = jnp.broadcast_to(taps[c : c + 1, :], (LANES, width))
            slid = pltpu.roll(line, 0, 1, stride=1, stride_axis=0)
            wt[c, pl.ds(k * LANES, LANES), :] = slid.astype(BF16)
    floor_row = jnp.concatenate(floor_rows, axis=1)
    norm_rows = [
        jnp.concatenate(
            [jnp.broadcast_to(inv_norm[k][c : c + 1, :], (1, LANES)) for k in range(share)], axis=1
        )
        for c in range(CHANNELS)
    ]

    station_at = lax.broadcasted_iota(jnp.int32, (GROUP, LANES), 0)
    lane_at = lax.broadcasted_iota(jnp.int32, (share * GROUP, LANES), 1)

    def column(value_at):
        col = jnp.zeros((GROUP, LANES), jnp.int32)
        for s in range(GROUP):
            col = jnp.where(station_at == s, value_at(s), col)
        return col

    def prepare(group):
        base = group * GROUP
        lag = jnp.concatenate(
            [column(lambda s, k=k: lags[first + k, base + s]) for k in range(share)], axis=0
        )
        region = column(lambda s: subnet[base + s])
        open_ = mask[pl.ds(base, GROUP), :].astype(F32)
        live = jnp.maximum(jnp.sum(open_, axis=1, keepdims=True), 1.0)
        return lag, region, open_ / live

    def work(group, ready):
        lag, region, weight = ready
        for o in range(owners):
            for half in range(2):
                block = recv[group * owners + o, half].astype(F32)
                for n in range(own_blocks):
                    ebuf[half * own_blocks + n, pl.ds(o * st_dev * PITCH, st_dev * PITCH), :] = block[
                        :, n * LANES : (n + 1) * LANES
                    ]

        def spread(parts):
            empty = jnp.zeros_like(parts[0])
            parts = parts + [empty] * (u_blocks + k_blocks - 1 - len(parts))
            return jnp.concatenate(
                [jnp.concatenate(parts[j : j + u_blocks], axis=0) for j in range(k_blocks)], axis=1
            )

        corr = []
        squares = []
        for c in range(CHANNELS):
            wave = [ebuf[n, pl.ds(c, GROUP, stride=PITCH), :] for n in range(2 * own_blocks)]
            corr.append(
                lax.dot_general(
                    spread([w.astype(BF16) for w in wave]), wt[c], NT_DIMS, preferred_element_type=F32
                )
            )
            high = [(w * w).astype(BF16) for w in wave]
            low = [(w * w - h.astype(F32)).astype(BF16) for w, h in zip(wave, high)]
            squares.append(spread(high))
            squares.append(spread(low))
        energy = lax.dot_general(
            jnp.concatenate(squares, axis=0), bt[...], NT_DIMS, preferred_element_type=F32
        )
        tall = u_blocks * GROUP
        coherent = None
        for c in range(CHANNELS):
            at = 2 * c * tall
            power = energy[at : at + tall] + energy[at + tall : at + 2 * tall]
            scale = jnp.concatenate([weight[:, c : c + 1]] * u_blocks, axis=0)
            term = corr[c] * lax.rsqrt(power + floor_row) * (scale * norm_rows[c])
            coherent = term if coherent is None else coherent + term

        pieces = [
            jnp.concatenate(
                [
                    coherent[b * GROUP : (b + 1) * GROUP, k * LANES : (k + 1) * LANES]
                    for k in range(share)
                ],
                axis=0,
            )
            for b in range(u_blocks)
        ]
        for bit in range(lag_bits):
            step = 1 << bit
            turned = [pltpu.roll(p, LANES - step, 1) for p in pieces]
            stays = lane_at < LANES - step
            taken = (lax.shift_right_logical(lag, bit) & 1) == 1
            pieces = [
                jnp.where(
                    taken, jnp.where(stays, turned[b], turned[min(b + 1, u_blocks - 1)]), pieces[b]
                )
                for b in range(u_blocks)
            ]
        for k in range(share):
            for r in range(REGIONS):
                member = region == r
                total = jnp.concatenate(
                    [
                        jnp.sum(
                            jnp.where(member, pieces[n][k * GROUP : (k + 1) * GROUP], 0.0),
                            axis=0,
                            keepdims=True,
                        )
                        for n in range(own_blocks)
                    ],
                    axis=1,
                )
                if n_groups == 1:
                    out[k, pl.ds(r, 1), :] = total
                else:
                    acc[k, pl.ds(r, 1), :] += total

    if n_groups == 1:
        ready = prepare(0)
        each(everyone - 1, lambda i: outgoing(i).wait_recv())
        work(0, ready)
    else:
        acc[...] = jnp.zeros_like(acc)
        each(everyone - 1, lambda i: outgoing(i).wait_recv())

        def one(group, carry):
            work(group, prepare(group))
            return carry

        lax.fori_loop(0, n_groups, one, 0)
        out[...] = acc[...]
    each(everyone - 1, lambda i: outgoing(i).wait_send())


def shards(traces, trace_tail, templates, win_lengths, moveouts, chan_mask, subnet):
    n_tmpl = lax.axis_size("tmpl")
    n_sta = lax.axis_size("sta")
    n_own = n_tmpl * n_sta
    st_dev, _, t_dev = traces.shape
    halo = trace_tail.shape[2]
    span = templates.shape[2]
    share = templates.shape[0] // n_sta
    width = ceil_div(LANES + span - 1, LANES) * LANES
    block = (st_dev * PITCH, t_dev)
    vmem = pl.BlockSpec(memory_space=pltpu.VMEM)
    smem = pl.BlockSpec(memory_space=pltpu.SMEM)
    return pl.pallas_call(
        functools.partial(kernel, n_sta, n_own, share),
        out_shape=jax.ShapeDtypeStruct((share, REGIONS, t_dev), F32),
        in_specs=[vmem, vmem, vmem, smem, smem, vmem, smem],
        out_specs=vmem,
        scratch_shapes=[
            pltpu.VMEM((2,) + block, F32),
            pltpu.VMEM((2,) + block, BF16),
            pltpu.VMEM((n_own, 2) + block, BF16),
            pltpu.VMEM((2 * t_dev // LANES, GROUP * PITCH, LANES), F32),
            pltpu.VMEM((share, 8, width), F32),
            pltpu.VMEM((CHANNELS, share * LANES, width), BF16),
            pltpu.VMEM((share * LANES, width), BF16),
            pltpu.VMEM((share, REGIONS, t_dev), F32),
            pltpu.SemaphoreType.DMA((2 * n_own - 1,)),
            pltpu.SemaphoreType.DMA((2 * n_own - 1,)),
        ],
        compiler_params=pltpu.CompilerParams(
            collective_id=0, has_side_effects=True, vmem_limit_bytes=32 * 1024 * 1024
        ),
        name="matched_filter",
    )(traces, trace_tail, templates, win_lengths, moveouts, chan_mask, subnet)


def solution(mesh):
    in_specs = (
        P(("tmpl", "sta"), None, ("parts", "sub")),
        P(("tmpl", "sta"), None, "parts"),
        P("tmpl", None, None),
        P(),
        P(),
        P("parts", None),
        P(),
    )
    out_specs = P(("tmpl", "sta"), None, ("parts", "sub"))
    return jax.shard_map(shards, mesh=mesh, in_specs=in_specs, out_specs=out_specs, check_vma=False)
```

```python
import functools

import jax
import jax.numpy as jnp
from jax import lax
from jax.experimental import pallas as pl
from jax.experimental.pallas import tpu as pltpu
from jax.sharding import PartitionSpec as P

REGIONS = 2
CHANNELS = 3
LANES = 128
GROUP = 16
F32 = jnp.float32
BF16 = jnp.bfloat16
NT_DIMS = (((1,), (1,)), ((), ()))


def ceil_div(a, b):
    return -(-a // b)


def each(count, body):
    if count <= 16:
        for i in range(count):
            body(i)
    else:
        lax.fori_loop(0, count, lambda i, c: (body(i), c)[1], 0)


def kernel(
    n_sta, n_own, share,
    traces_hbm, tail_hbm, templates_hbm, wins_hbm, lags_hbm, mask_hbm, subnet_hbm,
    out,
    tail, templates, wins, lags, mask, subnet,
    stage, send, recv, ebuf, tpad, wt, bt, acc, load_sem, send_sem, recv_sem,
):
    _, st_dev, t_dev = traces_hbm.shape
    halo = tail.shape[2]
    span = templates.shape[2]
    lag_bits = (halo - span).bit_length()
    own_blocks = t_dev // LANES
    u_blocks = ceil_div(t_dev + halo - span + 1, LANES)
    k_blocks = ceil_div(LANES + span - 1, LANES)
    width = k_blocks * LANES
    owners = GROUP // st_dev
    n_groups = n_own // owners
    everyone = 2 * n_own

    t_me = lax.axis_index("tmpl")
    a_me = lax.axis_index("sta")
    u_me = lax.axis_index("sub")
    own = t_me * n_sta + a_me
    flat = own * 2 + u_me

    def place(d):
        other = lax.rem(flat + d, everyone)
        return {"tmpl": other // (2 * n_sta), "sta": (other // 2) % n_sta, "sub": other % 2}

    pairs = [
        (traces_hbm, send.at[0]), (tail_hbm, tail), (templates_hbm, templates), (wins_hbm, wins),
        (lags_hbm, lags), (mask_hbm, mask), (subnet_hbm, subnet),
    ]
    loads = [pltpu.make_async_copy(a, b, load_sem.at[i]) for i, (a, b) in enumerate(pairs)]
    for load in loads:
        load.start()

    barrier = pltpu.get_barrier_semaphore()

    def greet(i):
        pl.semaphore_signal(barrier, inc=1, device_id=place(i + 1), device_id_type=pl.DeviceIdType.MESH)

    each(everyone - 1, greet)

    stage[...] = jnp.zeros_like(stage)
    tpad[...] = jnp.zeros_like(tpad)
    loads[0].wait()
    loads[1].wait()
    for c in range(CHANNELS):
        stage[c, :, pl.ds(0, halo)] = tail[c].astype(F32)
        main = send[0, c]
        recv[own, 0, c] = main
        send[1, c] = jnp.where(u_me == 1, main.astype(F32), stage[c]).astype(BF16)

    pl.semaphore_wait(barrier, everyone - 1)

    def outgoing(i):
        d = i + 1
        half = d % 2
        return pltpu.make_async_remote_copy(
            src_ref=send.at[half],
            dst_ref=recv.at[own, half],
            send_sem=send_sem.at[i],
            recv_sem=recv_sem.at[i],
            device_id=place(d),
            device_id_type=pl.DeviceIdType.MESH,
        )

    each(everyone - 1, lambda i: outgoing(i).start())

    for load in loads[2:]:
        load.wait()
    first = own * share

    def picked(values, at):
        lane = lax.broadcasted_iota(jnp.int32, values.shape, 1)
        return jnp.sum(jnp.where(lane == at, values, 0).astype(F32), axis=1, keepdims=True)

    row_at = lax.broadcasted_iota(jnp.int32, (LANES, width), 0)
    col_at = lax.broadcasted_iota(jnp.int32, (LANES, width), 1)
    apart = col_at - row_at
    floor_rows = []
    for k in range(share):
        win = picked(wins[...], first + k)
        floor_rows.append(jnp.broadcast_to(1e-05 * win, (1, LANES)))
        band = jnp.logical_and(apart >= 0, apart < win.astype(jnp.int32))
        bt[pl.ds(k * LANES, LANES), :] = jnp.where(band, 1.0, 0.0).astype(BF16)
    norm_rows = []
    for c in range(CHANNELS):
        tpad[c, :, pl.ds(0, span)] = templates[c].astype(F32)
        norms = []
        for k in range(share):
            taps = tpad[c, pl.ds(a_me * share + k, 1), :]
            power = jnp.sum(taps * taps, axis=1, keepdims=True)
            norms.append(jnp.broadcast_to(1.0 / jnp.sqrt(power + 1e-06), (1, LANES)))
            line = jnp.broadcast_to(taps, (LANES, width))
            slid = pltpu.roll(line, 0, 1, stride=1, stride_axis=0)
            wt[c, pl.ds(k * LANES, LANES), :] = slid.astype(BF16)
        norm_rows.append(jnp.concatenate(norms, axis=1))
    floor_row = jnp.concatenate(floor_rows, axis=1)

    lane_at = lax.broadcasted_iota(jnp.int32, (share * GROUP, LANES), 1)

    def prepare(group):
        base = group * GROUP
        rows = lags[pl.ds(base, GROUP), :]
        lag = jnp.concatenate([picked(rows, first + k) for k in range(share)], axis=0)
        lag = jnp.broadcast_to(lag.astype(jnp.int32), (share * GROUP, LANES))
        square = (GROUP, subnet.shape[1])
        here = lax.broadcasted_iota(jnp.int32, square, 1) == base + lax.broadcasted_iota(
            jnp.int32, square, 0
        )

        def column(row):
            spread_row = jnp.broadcast_to(row.astype(F32), square)
            return jnp.sum(jnp.where(here, spread_row, 0.0), axis=1, keepdims=True)

        region = jnp.broadcast_to(column(subnet[...]).astype(jnp.int32), (GROUP, LANES))
        open_ = [column(mask[pl.ds(c, 1), :]) for c in range(CHANNELS)]
        live = jnp.maximum(functools.reduce(jnp.add, open_), 1.0)
        return lag, region, [o / live for o in open_]

    def work(group, ready):
        lag, region, weight = ready
        for o in range(owners):
            for half in range(2):
                for c in range(CHANNELS):
                    block = recv[group * owners + o, half, c].astype(F32)
                    for n in range(own_blocks):
                        ebuf[c, half * own_blocks + n, pl.ds(o * st_dev, st_dev), :] = block[
                            :, n * LANES : (n + 1) * LANES
                        ]

        def spread(parts):
            empty = jnp.zeros_like(parts[0])
            parts = parts + [empty] * (u_blocks + k_blocks - 1 - len(parts))
            return jnp.concatenate(
                [jnp.concatenate(parts[j : j + u_blocks], axis=0) for j in range(k_blocks)], axis=1
            )

        corr = []
        squares = []
        for c in range(CHANNELS):
            wave = [ebuf[c, n] for n in range(2 * own_blocks)]
            corr.append(
                lax.dot_general(
                    spread([w.astype(BF16) for w in wave]), wt[c], NT_DIMS, preferred_element_type=F32
                )
            )
            high = [(w * w).astype(BF16) for w in wave]
            low = [(w * w - h.astype(F32)).astype(BF16) for w, h in zip(wave, high)]
            squares.append(spread(high))
            squares.append(spread(low))
        energy = lax.dot_general(
            jnp.concatenate(squares, axis=0), bt[...], NT_DIMS, preferred_element_type=F32
        )
        tall = u_blocks * GROUP
        coherent = None
        for c in range(CHANNELS):
            at = 2 * c * tall
            power = energy[at : at + tall] + energy[at + tall : at + 2 * tall]
            scale = jnp.concatenate([weight[c]] * u_blocks, axis=0)
            term = corr[c] * lax.rsqrt(power + floor_row) * (scale * norm_rows[c])
            coherent = term if coherent is None else coherent + term

        pieces = [
            jnp.concatenate(
                [
                    coherent[b * GROUP : (b + 1) * GROUP, k * LANES : (k + 1) * LANES]
                    for k in range(share)
                ],
                axis=0,
            )
            for b in range(u_blocks)
        ]
        for bit in range(lag_bits):
            step = 1 << bit
            turned = [pltpu.roll(p, LANES - step, 1) for p in pieces]
            stays = lane_at < LANES - step
            taken = (lax.shift_right_logical(lag, bit) & 1) == 1
            pieces = [
                jnp.where(
                    taken, jnp.where(stays, turned[b], turned[min(b + 1, u_blocks - 1)]), pieces[b]
                )
                for b in range(u_blocks)
            ]
        for k in range(share):
            for r in range(REGIONS):
                member = region == r
                total = jnp.concatenate(
                    [
                        jnp.sum(
                            jnp.where(member, pieces[n][k * GROUP : (k + 1) * GROUP], 0.0),
                            axis=0,
                            keepdims=True,
                        )
                        for n in range(own_blocks)
                    ],
                    axis=1,
                )
                if n_groups == 1:
                    out[k, pl.ds(r, 1), :] = total
                else:
                    acc[k, pl.ds(r, 1), :] += total

    if n_groups == 1:
        ready = prepare(0)
        each(everyone - 1, lambda i: outgoing(i).wait_recv())
        work(0, ready)
    else:
        acc[...] = jnp.zeros_like(acc)
        each(everyone - 1, lambda i: outgoing(i).wait_recv())

        def one(group, carry):
            work(group, prepare(group))
            return carry

        lax.fori_loop(0, n_groups, one, 0)
        out[...] = acc[...]
    each(everyone - 1, lambda i: outgoing(i).wait_send())


def shards(traces, trace_tail, templates, win_lengths, moveouts, chan_mask, subnet):
    n_tmpl = lax.axis_size("tmpl")
    n_sta = lax.axis_size("sta")
    n_own = n_tmpl * n_sta
    st_dev, _, t_dev = traces.shape
    share = templates.shape[0] // n_sta
    span = templates.shape[2]
    width = ceil_div(LANES + span - 1, LANES) * LANES
    block = (CHANNELS, st_dev, t_dev)
    operands = (
        jnp.transpose(traces, (1, 0, 2)),
        jnp.transpose(trace_tail, (1, 0, 2)),
        jnp.transpose(templates, (1, 0, 2)),
        win_lengths.reshape(1, -1),
        moveouts.T,
        chan_mask.T,
        subnet.reshape(1, -1),
    )
    return pl.pallas_call(
        functools.partial(kernel, n_sta, n_own, share),
        out_shape=jax.ShapeDtypeStruct((share, REGIONS, t_dev), F32),
        in_specs=[pl.BlockSpec(memory_space=pltpu.HBM)] * len(operands),
        out_specs=pl.BlockSpec(memory_space=pltpu.VMEM),
        scratch_shapes=[pltpu.VMEM(x.shape, x.dtype) for x in operands[1:]]
        + [
            pltpu.VMEM(block, F32),
            pltpu.VMEM((2,) + block, BF16),
            pltpu.VMEM((n_own, 2) + block, BF16),
            pltpu.VMEM((CHANNELS, 2 * t_dev // LANES, GROUP, LANES), F32),
            pltpu.VMEM((CHANNELS, templates.shape[0], width), F32),
            pltpu.VMEM((CHANNELS, share * LANES, width), BF16),
            pltpu.VMEM((share * LANES, width), BF16),
            pltpu.VMEM((share, REGIONS, t_dev), F32),
            pltpu.SemaphoreType.DMA((len(operands),)),
            pltpu.SemaphoreType.DMA((2 * n_own - 1,)),
            pltpu.SemaphoreType.DMA((2 * n_own - 1,)),
        ],
        compiler_params=pltpu.CompilerParams(
            collective_id=0, has_side_effects=True, vmem_limit_bytes=60 * 1024 * 1024
        ),
        name="matched_filter",
    )(*operands)


def solution(mesh):
    in_specs = (
        P(("tmpl", "sta"), None, ("parts", "sub")),
        P(("tmpl", "sta"), None, "parts"),
        P("tmpl", None, None),
        P(),
        P(),
        P("parts", None),
        P(),
    )
    out_specs = P(("tmpl", "sta"), None, ("parts", "sub"))
    return jax.shard_map(shards, mesh=mesh, in_specs=in_specs, out_specs=out_specs, check_vma=False)
```

```python
import functools

import jax
import jax.numpy as jnp
from jax import lax
from jax.experimental import pallas as pl
from jax.experimental.pallas import tpu as pltpu
from jax.sharding import PartitionSpec as P

REGIONS = 2
CHANNELS = 3
LANES = 128
GROUP = 16
F32 = jnp.float32
BF16 = jnp.bfloat16
NT_DIMS = (((1,), (1,)), ((), ()))


def ceil_div(a, b):
    return -(-a // b)


def each(count, body):
    if count <= 16:
        for i in range(count):
            body(i)
    else:
        lax.fori_loop(0, count, lambda i, c: (body(i), c)[1], 0)


def kernel(
    n_sta, n_own, share,
    traces_hbm, tail_hbm, templates_hbm, wins_hbm, lags_hbm, mask_hbm, subnet_hbm,
    out,
    tail, templates, wins, lags, mask, subnet,
    stage, send, recv, ebuf, tpad, wt, bt, acc, load_sem, send_sem, recv_sem,
):
    _, st_dev, t_dev = traces_hbm.shape
    halo = tail.shape[2]
    span = templates.shape[2]
    lag_bits = (halo - span).bit_length()
    own_blocks = t_dev // LANES
    u_blocks = ceil_div(t_dev + halo - span + 1, LANES)
    k_blocks = ceil_div(LANES + span - 1, LANES)
    width = k_blocks * LANES
    owners = GROUP // st_dev
    n_groups = n_own // owners
    everyone = 2 * n_own

    t_me = lax.axis_index("tmpl")
    a_me = lax.axis_index("sta")
    u_me = lax.axis_index("sub")
    own = t_me * n_sta + a_me
    flat = own * 2 + u_me

    def place(d):
        other = lax.rem(flat + d, everyone)
        return {"tmpl": other // (2 * n_sta), "sta": (other // 2) % n_sta, "sub": other % 2}

    pairs = [
        (traces_hbm, send.at[0]), (tail_hbm, tail), (templates_hbm, templates), (wins_hbm, wins),
        (lags_hbm, lags), (mask_hbm, mask), (subnet_hbm, subnet),
    ]
    loads = [pltpu.make_async_copy(a, b, load_sem.at[i]) for i, (a, b) in enumerate(pairs)]
    for load in loads:
        load.start()

    barrier = pltpu.get_barrier_semaphore()

    def greet(i):
        pl.semaphore_signal(barrier, inc=1, device_id=place(i + 1), device_id_type=pl.DeviceIdType.MESH)

    each(everyone - 1, greet)

    stage[...] = jnp.zeros_like(stage)
    tpad[...] = jnp.zeros_like(tpad)
    loads[0].wait()
    loads[1].wait()
    for c in range(CHANNELS):
        stage[c, :, pl.ds(0, halo)] = tail[c].astype(F32)
        main = send[0, c]
        recv[own, 0, c] = main
        send[1, c] = jnp.where(u_me == 1, main.astype(F32), stage[c]).astype(BF16)

    pl.semaphore_wait(barrier, everyone - 1)

    def outgoing(i):
        d = i + 1
        half = d % 2
        return pltpu.make_async_remote_copy(
            src_ref=send.at[half],
            dst_ref=recv.at[own, half],
            send_sem=send_sem.at[i],
            recv_sem=recv_sem.at[i],
            device_id=place(d),
            device_id_type=pl.DeviceIdType.MESH,
        )

    order = sorted(range(everyone - 1), key=lambda i: abs(i + 1 - n_own))
    if n_groups == 1:
        for i in order:
            outgoing(i).start()
    else:
        each(everyone - 1, lambda i: outgoing(i).start())

    for load in loads[2:]:
        load.wait()
    first = own * share

    def picked(values, at):
        lane = lax.broadcasted_iota(jnp.int32, values.shape, 1)
        return jnp.sum(jnp.where(lane == at, values, 0).astype(F32), axis=1, keepdims=True)

    row_at = lax.broadcasted_iota(jnp.int32, (LANES, width), 0)
    col_at = lax.broadcasted_iota(jnp.int32, (LANES, width), 1)
    apart = col_at - row_at
    floor_rows = []
    for k in range(share):
        win = picked(wins[...], first + k)
        floor_rows.append(jnp.broadcast_to(1e-05 * win, (1, LANES)))
        band = jnp.logical_and(apart >= 0, apart < win.astype(jnp.int32))
        bt[pl.ds(k * LANES, LANES), :] = jnp.where(band, 1.0, 0.0).astype(BF16)
    norm_rows = []
    for c in range(CHANNELS):
        tpad[c, :, pl.ds(0, span)] = templates[c].astype(F32)
        norms = []
        for k in range(share):
            taps = tpad[c, pl.ds(a_me * share + k, 1), :]
            power = jnp.sum(taps * taps, axis=1, keepdims=True)
            norms.append(jnp.broadcast_to(1.0 / jnp.sqrt(power + 1e-06), (1, LANES)))
            line = jnp.broadcast_to(taps, (LANES, width))
            slid = pltpu.roll(line, 0, 1, stride=1, stride_axis=0)
            wt[c, pl.ds(k * LANES, LANES), :] = slid.astype(BF16)
        norm_rows.append(jnp.concatenate(norms, axis=1))
    floor_row = jnp.concatenate(floor_rows, axis=1)

    lane_at = lax.broadcasted_iota(jnp.int32, (share * GROUP, LANES), 1)

    def prepare(group):
        base = group * GROUP
        rows = lags[pl.ds(base, GROUP), :]
        lag = jnp.concatenate([picked(rows, first + k) for k in range(share)], axis=0)
        lag = jnp.broadcast_to(lag.astype(jnp.int32), (share * GROUP, LANES))
        square = (GROUP, subnet.shape[1])
        here = lax.broadcasted_iota(jnp.int32, square, 1) == base + lax.broadcasted_iota(
            jnp.int32, square, 0
        )

        def column(row):
            spread_row = jnp.broadcast_to(row.astype(F32), square)
            return jnp.sum(jnp.where(here, spread_row, 0.0), axis=1, keepdims=True)

        region = jnp.broadcast_to(column(subnet[...]).astype(jnp.int32), (GROUP, LANES))
        open_ = [column(mask[pl.ds(c, 1), :]) for c in range(CHANNELS)]
        live = jnp.maximum(functools.reduce(jnp.add, open_), 1.0)
        return lag, region, [o / live for o in open_]

    def work(group, ready):
        lag, region, weight = ready
        for o in range(owners):
            for half in range(2):
                for c in range(CHANNELS):
                    block = recv[group * owners + o, half, c].astype(F32)
                    for n in range(own_blocks):
                        ebuf[c, half * own_blocks + n, pl.ds(o * st_dev, st_dev), :] = block[
                            :, n * LANES : (n + 1) * LANES
                        ]

        def spread(parts):
            empty = jnp.zeros_like(parts[0])
            parts = parts + [empty] * (u_blocks + k_blocks - 1 - len(parts))
            return jnp.concatenate(
                [jnp.concatenate(parts[j : j + u_blocks], axis=0) for j in range(k_blocks)], axis=1
            )

        corr = []
        squares = []
        for c in range(CHANNELS):
            wave = [ebuf[c, n] for n in range(2 * own_blocks)]
            corr.append(
                lax.dot_general(
                    spread([w.astype(BF16) for w in wave]), wt[c], NT_DIMS, preferred_element_type=F32
                )
            )
            high = [(w * w).astype(BF16) for w in wave]
            low = [(w * w - h.astype(F32)).astype(BF16) for w, h in zip(wave, high)]
            squares.append(spread(high))
            squares.append(spread(low))
        energy = lax.dot_general(
            jnp.concatenate(squares, axis=0), bt[...], NT_DIMS, preferred_element_type=F32
        )
        tall = u_blocks * GROUP
        coherent = None
        for c in range(CHANNELS):
            at = 2 * c * tall
            power = energy[at : at + tall] + energy[at + tall : at + 2 * tall]
            scale = jnp.concatenate([weight[c]] * u_blocks, axis=0)
            term = corr[c] * lax.rsqrt(power + floor_row) * (scale * norm_rows[c])
            coherent = term if coherent is None else coherent + term

        pieces = [
            jnp.concatenate(
                [
                    coherent[b * GROUP : (b + 1) * GROUP, k * LANES : (k + 1) * LANES]
                    for k in range(share)
                ],
                axis=0,
            )
            for b in range(u_blocks)
        ]
        for bit in range(lag_bits):
            step = 1 << bit
            turned = [pltpu.roll(p, LANES - step, 1) for p in pieces]
            stays = lane_at < LANES - step
            taken = (lax.shift_right_logical(lag, bit) & 1) == 1
            pieces = [
                jnp.where(
                    taken, jnp.where(stays, turned[b], turned[min(b + 1, u_blocks - 1)]), pieces[b]
                )
                for b in range(u_blocks)
            ]
        for k in range(share):
            for r in range(REGIONS):
                member = region == r
                total = jnp.concatenate(
                    [
                        jnp.sum(
                            jnp.where(member, pieces[n][k * GROUP : (k + 1) * GROUP], 0.0),
                            axis=0,
                            keepdims=True,
                        )
                        for n in range(own_blocks)
                    ],
                    axis=1,
                )
                if n_groups == 1:
                    out[k, pl.ds(r, 1), :] = total
                else:
                    acc[k, pl.ds(r, 1), :] += total

    if n_groups == 1:
        ready = prepare(0)
        each(everyone - 1, lambda i: outgoing(i).wait_recv())
        work(0, ready)
    else:
        acc[...] = jnp.zeros_like(acc)
        each(everyone - 1, lambda i: outgoing(i).wait_recv())

        def one(group, carry):
            work(group, prepare(group))
            return carry

        lax.fori_loop(0, n_groups, one, 0)
        out[...] = acc[...]
    each(everyone - 1, lambda i: outgoing(i).wait_send())


def shards(traces, trace_tail, templates, win_lengths, moveouts, chan_mask, subnet):
    n_tmpl = lax.axis_size("tmpl")
    n_sta = lax.axis_size("sta")
    n_own = n_tmpl * n_sta
    st_dev, _, t_dev = traces.shape
    share = templates.shape[0] // n_sta
    span = templates.shape[2]
    width = ceil_div(LANES + span - 1, LANES) * LANES
    block = (CHANNELS, st_dev, t_dev)
    operands = (
        jnp.transpose(traces, (1, 0, 2)),
        jnp.transpose(trace_tail, (1, 0, 2)),
        jnp.transpose(templates, (1, 0, 2)),
        win_lengths.reshape(1, -1),
        moveouts.T,
        chan_mask.T,
        subnet.reshape(1, -1),
    )
    return pl.pallas_call(
        functools.partial(kernel, n_sta, n_own, share),
        out_shape=jax.ShapeDtypeStruct((share, REGIONS, t_dev), F32),
        in_specs=[pl.BlockSpec(memory_space=pltpu.HBM)] * len(operands),
        out_specs=pl.BlockSpec(memory_space=pltpu.VMEM),
        scratch_shapes=[pltpu.VMEM(x.shape, x.dtype) for x in operands[1:]]
        + [
            pltpu.VMEM(block, F32),
            pltpu.VMEM((2,) + block, BF16),
            pltpu.VMEM((n_own, 2) + block, BF16),
            pltpu.VMEM((CHANNELS, 2 * t_dev // LANES, GROUP, LANES), F32),
            pltpu.VMEM((CHANNELS, templates.shape[0], width), F32),
            pltpu.VMEM((CHANNELS, share * LANES, width), BF16),
            pltpu.VMEM((share * LANES, width), BF16),
            pltpu.VMEM((share, REGIONS, t_dev), F32),
            pltpu.SemaphoreType.DMA((len(operands),)),
            pltpu.SemaphoreType.DMA((2 * n_own - 1,)),
            pltpu.SemaphoreType.DMA((2 * n_own - 1,)),
        ],
        compiler_params=pltpu.CompilerParams(
            collective_id=0, has_side_effects=True, vmem_limit_bytes=32 * 1024 * 1024
        ),
        name="matched_filter",
    )(*(pltpu.with_memory_space_constraint(x, pltpu.HBM) for x in operands))


def solution(mesh):
    in_specs = (
        P(("tmpl", "sta"), None, ("parts", "sub")),
        P(("tmpl", "sta"), None, "parts"),
        P("tmpl", None, None),
        P(),
        P(),
        P("parts", None),
        P(),
    )
    out_specs = P(("tmpl", "sta"), None, ("parts", "sub"))
    return jax.shard_map(shards, mesh=mesh, in_specs=in_specs, out_specs=out_specs, check_vma=False)
```

```python
import functools

import jax
import jax.numpy as jnp
from jax import lax
from jax.experimental import pallas as pl
from jax.experimental.pallas import tpu as pltpu
from jax.sharding import PartitionSpec as P

REGIONS = 2
CHANNELS = 3
LANES = 128
GROUP = 16
F32 = jnp.float32
BF16 = jnp.bfloat16


def ceil_div(a, b):
    return -(-a // b)


def each(count, body):
    if count <= 16:
        for i in range(count):
            body(i)
    else:
        lax.fori_loop(0, count, lambda i, c: (body(i), c)[1], 0)


def kernel(
    n_sta, n_own, share,
    traces_hbm, tail_hbm, templates_hbm, wins_hbm, lags_hbm, mask_hbm, subnet_hbm,
    out,
    tail, templates, wins, lags, mask, subnet,
    stage, send, recv, ebuf, tpad, lines, wt, bt, acc, load_sem, send_sem, recv_sem,
):
    _, st_dev, t_dev = traces_hbm.shape
    halo = tail.shape[2]
    span = templates.shape[2]
    lag_bits = (halo - span).bit_length()
    own_blocks = t_dev // LANES
    u_blocks = ceil_div(t_dev + halo - span + 1, LANES)
    k_blocks = ceil_div(LANES + span - 1, LANES)
    width = k_blocks * LANES
    owners = GROUP // st_dev
    n_groups = n_own // owners
    everyone = 2 * n_own

    t_me = lax.axis_index("tmpl")
    a_me = lax.axis_index("sta")
    u_me = lax.axis_index("sub")
    own = t_me * n_sta + a_me
    flat = own * 2 + u_me

    def place(d):
        other = lax.rem(flat + d, everyone)
        return {"tmpl": other // (2 * n_sta), "sta": (other // 2) % n_sta, "sub": other % 2}

    pairs = [
        (traces_hbm, send.at[0]), (tail_hbm, tail), (templates_hbm, templates), (wins_hbm, wins),
        (lags_hbm, lags), (mask_hbm, mask), (subnet_hbm, subnet),
    ]
    loads = [pltpu.make_async_copy(a, b, load_sem.at[i]) for i, (a, b) in enumerate(pairs)]
    for load in loads:
        load.start()

    barrier = pltpu.get_barrier_semaphore()

    def greet(i):
        pl.semaphore_signal(barrier, inc=1, device_id=place(i + 1), device_id_type=pl.DeviceIdType.MESH)

    each(everyone - 1, greet)

    stage[...] = jnp.zeros_like(stage)
    tpad[...] = jnp.zeros_like(tpad)
    loads[0].wait()
    loads[1].wait()
    for c in range(CHANNELS):
        stage[c, :, pl.ds(0, halo)] = tail[c].astype(F32)
        main = send[0, c]
        recv[own, 0, c] = main
        send[1, c] = jnp.where(u_me == 1, main.astype(F32), stage[c]).astype(BF16)

    pl.semaphore_wait(barrier, everyone - 1)

    def outgoing(i):
        d = i + 1
        half = d % 2
        return pltpu.make_async_remote_copy(
            src_ref=send.at[half],
            dst_ref=recv.at[own, half],
            send_sem=send_sem.at[i],
            recv_sem=recv_sem.at[i],
            device_id=place(d),
            device_id_type=pl.DeviceIdType.MESH,
        )

    order = sorted(range(everyone - 1), key=lambda i: abs(i + 1 - n_own))
    if n_groups == 1:
        for i in order:
            outgoing(i).start()
    else:
        each(everyone - 1, lambda i: outgoing(i).start())

    for load in loads[2:]:
        load.wait()
    first = own * share

    def picked(values, at):
        lane = lax.broadcasted_iota(jnp.int32, values.shape, 1)
        return jnp.sum(jnp.where(lane == at, values, 0).astype(F32), axis=1, keepdims=True)

    row_at = lax.broadcasted_iota(jnp.int32, (width, LANES), 0)
    col_at = lax.broadcasted_iota(jnp.int32, (width, LANES), 1)
    apart = row_at - col_at
    floor_rows = []
    for k in range(share):
        win = picked(wins[...], first + k)
        floor_rows.append(jnp.broadcast_to(1e-05 * win, (1, LANES)))
        band = jnp.logical_and(apart >= 0, apart < win.astype(jnp.int32))
        bt[:, pl.ds(k * LANES, LANES)] = jnp.where(band, 1.0, 0.0).astype(BF16)
    mirror = lax.broadcasted_iota(jnp.int32, (width, width), 0) + lax.broadcasted_iota(
        jnp.int32, (width, width), 1
    )
    mirror = jnp.where(mirror == span - 1, 1.0, 0.0).astype(BF16)
    k_dev = templates.shape[1]
    for c in range(CHANNELS):
        tpad[c, :, pl.ds(0, span)] = templates[c].astype(F32)
    mirrored = jnp.dot(
        jnp.concatenate([tpad[c] for c in range(CHANNELS)], axis=0).astype(BF16),
        mirror,
        preferred_element_type=F32,
    )
    norm_rows = []
    for c in range(CHANNELS):
        norms = []
        for k in range(share):
            taps = tpad[c, pl.ds(a_me * share + k, 1), :]
            power = jnp.sum(taps * taps, axis=1, keepdims=True)
            norms.append(jnp.broadcast_to(1.0 / jnp.sqrt(power + 1e-06), (1, LANES)))
        norm_rows.append(jnp.concatenate(norms, axis=1))
        for j in range(k_blocks):
            turned = pltpu.roll(
                mirrored[c * k_dev : (c + 1) * k_dev], (j * LANES - span + 1) % width, 1
            )
            lines[c, j] = jnp.concatenate([turned[:, :LANES], turned[:, width - LANES :]], axis=1)
            for k in range(share):
                line = lines[c, j, pl.ds(a_me * share + k, 1), :]
                slid = pltpu.roll(
                    jnp.broadcast_to(line, (LANES, 2 * LANES)), 0, 1, stride=1, stride_axis=0
                )
                wt[c, pl.ds(j * LANES, LANES), pl.ds(k * LANES, LANES)] = slid[:, :LANES].astype(BF16)
    floor_row = jnp.concatenate(floor_rows, axis=1)

    lane_at = lax.broadcasted_iota(jnp.int32, (share * GROUP, LANES), 1)

    def prepare(group):
        base = group * GROUP
        rows = lags[pl.ds(base, GROUP), :]
        lag = jnp.concatenate([picked(rows, first + k) for k in range(share)], axis=0)
        lag = jnp.broadcast_to(lag.astype(jnp.int32), (share * GROUP, LANES))
        square = (GROUP, subnet.shape[1])
        here = lax.broadcasted_iota(jnp.int32, square, 1) == base + lax.broadcasted_iota(
            jnp.int32, square, 0
        )

        def column(row):
            spread_row = jnp.broadcast_to(row.astype(F32), square)
            return jnp.sum(jnp.where(here, spread_row, 0.0), axis=1, keepdims=True)

        region = jnp.broadcast_to(column(subnet[...]).astype(jnp.int32), (GROUP, LANES))
        open_ = [column(mask[pl.ds(c, 1), :]) for c in range(CHANNELS)]
        live = jnp.maximum(functools.reduce(jnp.add, open_), 1.0)
        return lag, region, [o / live for o in open_]

    def work(group, ready):
        lag, region, weight = ready
        for o in range(owners):
            for half in range(2):
                for c in range(CHANNELS):
                    block = recv[group * owners + o, half, c].astype(F32)
                    for n in range(own_blocks):
                        ebuf[c, half * own_blocks + n, pl.ds(o * st_dev, st_dev), :] = block[
                            :, n * LANES : (n + 1) * LANES
                        ]

        def spread(parts):
            empty = jnp.zeros_like(parts[0])
            parts = parts + [empty] * (u_blocks + k_blocks - 1 - len(parts))
            return jnp.concatenate(
                [jnp.concatenate(parts[j : j + u_blocks], axis=0) for j in range(k_blocks)], axis=1
            )

        corr = []
        squares = []
        for c in range(CHANNELS):
            wave = [ebuf[c, n] for n in range(2 * own_blocks)]
            corr.append(
                jnp.dot(spread([w.astype(BF16) for w in wave]), wt[c], preferred_element_type=F32)
            )
            high = [(w * w).astype(BF16) for w in wave]
            low = [(w * w - h.astype(F32)).astype(BF16) for w, h in zip(wave, high)]
            squares.append(spread(high))
            squares.append(spread(low))
        energy = jnp.dot(
            jnp.concatenate(squares, axis=0), bt[...], preferred_element_type=F32
        )
        tall = u_blocks * GROUP
        coherent = None
        for c in range(CHANNELS):
            at = 2 * c * tall
            power = energy[at : at + tall] + energy[at + tall : at + 2 * tall]
            scale = jnp.concatenate([weight[c]] * u_blocks, axis=0)
            term = corr[c] * lax.rsqrt(power + floor_row) * (scale * norm_rows[c])
            coherent = term if coherent is None else coherent + term

        pieces = [
            jnp.concatenate(
                [
                    coherent[b * GROUP : (b + 1) * GROUP, k * LANES : (k + 1) * LANES]
                    for k in range(share)
                ],
                axis=0,
            )
            for b in range(u_blocks)
        ]
        for bit in range(lag_bits):
            step = 1 << bit
            turned = [pltpu.roll(p, LANES - step, 1) for p in pieces]
            stays = lane_at < LANES - step
            taken = (lax.shift_right_logical(lag, bit) & 1) == 1
            pieces = [
                jnp.where(
                    taken, jnp.where(stays, turned[b], turned[min(b + 1, u_blocks - 1)]), pieces[b]
                )
                for b in range(u_blocks)
            ]
        for k in range(share):
            for r in range(REGIONS):
                member = region == r
                total = jnp.concatenate(
                    [
                        jnp.sum(
                            jnp.where(member, pieces[n][k * GROUP : (k + 1) * GROUP], 0.0),
                            axis=0,
                            keepdims=True,
                        )
                        for n in range(own_blocks)
                    ],
                    axis=1,
                )
                if n_groups == 1:
                    out[k, pl.ds(r, 1), :] = total
                else:
                    acc[k, pl.ds(r, 1), :] += total

    if n_groups == 1:
        ready = prepare(0)
        each(everyone - 1, lambda i: outgoing(i).wait_recv())
        work(0, ready)
    else:
        acc[...] = jnp.zeros_like(acc)
        each(everyone - 1, lambda i: outgoing(i).wait_recv())

        def one(group, carry):
            work(group, prepare(group))
            return carry

        lax.fori_loop(0, n_groups, one, 0)
        out[...] = acc[...]
    each(everyone - 1, lambda i: outgoing(i).wait_send())


def shards(traces, trace_tail, templates, win_lengths, moveouts, chan_mask, subnet):
    n_tmpl = lax.axis_size("tmpl")
    n_sta = lax.axis_size("sta")
    n_own = n_tmpl * n_sta
    st_dev, _, t_dev = traces.shape
    share = templates.shape[0] // n_sta
    span = templates.shape[2]
    width = ceil_div(LANES + span - 1, LANES) * LANES
    block = (CHANNELS, st_dev, t_dev)
    operands = (
        jnp.transpose(traces, (1, 0, 2)),
        jnp.transpose(trace_tail, (1, 0, 2)),
        jnp.transpose(templates, (1, 0, 2)),
        win_lengths.reshape(1, -1),
        moveouts.T,
        chan_mask.T,
        subnet.reshape(1, -1),
    )
    return pl.pallas_call(
        functools.partial(kernel, n_sta, n_own, share),
        out_shape=jax.ShapeDtypeStruct((share, REGIONS, t_dev), F32),
        in_specs=[pl.BlockSpec(memory_space=pltpu.HBM)] * len(operands),
        out_specs=pl.BlockSpec(memory_space=pltpu.VMEM),
        scratch_shapes=[pltpu.VMEM(x.shape, x.dtype) for x in operands[1:]]
        + [
            pltpu.VMEM(block, F32),
            pltpu.VMEM((2,) + block, BF16),
            pltpu.VMEM((n_own, 2) + block, BF16),
            pltpu.VMEM((CHANNELS, 2 * t_dev // LANES, GROUP, LANES), F32),
            pltpu.VMEM((CHANNELS, templates.shape[0], width), F32),
            pltpu.VMEM((CHANNELS, width // LANES, templates.shape[0], 2 * LANES), F32),
            pltpu.VMEM((CHANNELS, width, share * LANES), BF16),
            pltpu.VMEM((width, share * LANES), BF16),
            pltpu.VMEM((share, REGIONS, t_dev), F32),
            pltpu.SemaphoreType.DMA((len(operands),)),
            pltpu.SemaphoreType.DMA((2 * n_own - 1,)),
            pltpu.SemaphoreType.DMA((2 * n_own - 1,)),
        ],
        compiler_params=pltpu.CompilerParams(
            collective_id=0, has_side_effects=True, vmem_limit_bytes=32 * 1024 * 1024
        ),
        name="matched_filter",
    )(*(pltpu.with_memory_space_constraint(x, pltpu.HBM) for x in operands))


def solution(mesh):
    in_specs = (
        P(("tmpl", "sta"), None, ("parts", "sub")),
        P(("tmpl", "sta"), None, "parts"),
        P("tmpl", None, None),
        P(),
        P(),
        P("parts", None),
        P(),
    )
    out_specs = P(("tmpl", "sta"), None, ("parts", "sub"))
    return jax.shard_map(shards, mesh=mesh, in_specs=in_specs, out_specs=out_specs, check_vma=False)
```

```python
import functools

import jax
import jax.numpy as jnp
from jax import lax
from jax.experimental import pallas as pl
from jax.experimental.pallas import tpu as pltpu
from jax.sharding import PartitionSpec as P

REGIONS = 2
CHANNELS = 3
LANES = 128
GROUP = 16
F32 = jnp.float32
BF16 = jnp.bfloat16


def ceil_div(a, b):
    return -(-a // b)


def each(count, body):
    if count <= 16:
        for i in range(count):
            body(i)
    else:
        lax.fori_loop(0, count, lambda i, c: (body(i), c)[1], 0)


def kernel(
    n_sta, n_own, share,
    traces_hbm, tail_hbm, templates_hbm, wins_hbm, lags_hbm, mask_hbm, subnet_hbm,
    out,
    tail, templates, wins, lags, mask, subnet,
    stage, send, recv, ebuf, tpad, lines, wt, bt, acc, load_sem, send_sem, recv_sem,
):
    _, st_dev, t_dev = traces_hbm.shape
    halo = tail.shape[2]
    span = templates.shape[2]
    lag_bits = (halo - span).bit_length()
    own_blocks = t_dev // LANES
    u_blocks = ceil_div(t_dev + halo - span + 1, LANES)
    k_blocks = ceil_div(LANES + span - 1, LANES)
    width = k_blocks * LANES
    owners = GROUP // st_dev
    n_groups = n_own // owners
    everyone = 2 * n_own

    t_me = lax.axis_index("tmpl")
    a_me = lax.axis_index("sta")
    u_me = lax.axis_index("sub")
    own = t_me * n_sta + a_me

    def place(d):
        if isinstance(d, int):
            d_t, d_a, d_u = d // (2 * n_sta), d // 2 % n_sta, d % 2
        else:
            d_t, d_a, d_u = lax.div(d, 2 * n_sta), lax.rem(lax.div(d, 2), n_sta), lax.rem(d, 2)
        return {
            "tmpl": lax.rem(t_me + d_t, n_own // n_sta),
            "sta": lax.rem(a_me + d_a, n_sta),
            "sub": lax.rem(u_me + d_u, 2),
        }

    pairs = [
        (traces_hbm, send.at[0]), (tail_hbm, tail), (templates_hbm, templates), (wins_hbm, wins),
        (lags_hbm, lags), (mask_hbm, mask), (subnet_hbm, subnet),
    ]
    loads = [pltpu.make_async_copy(a, b, load_sem.at[i]) for i, (a, b) in enumerate(pairs)]
    for load in loads:
        load.start()

    barrier = pltpu.get_barrier_semaphore()

    def greet(i):
        pl.semaphore_signal(barrier, inc=1, device_id=place(i + 1), device_id_type=pl.DeviceIdType.MESH)

    each(everyone - 1, greet)

    stage[...] = jnp.zeros_like(stage)
    tpad[...] = jnp.zeros_like(tpad)
    loads[0].wait()
    loads[1].wait()
    for c in range(CHANNELS):
        stage[c, :, pl.ds(0, halo)] = tail[c].astype(F32)
        main = send[0, c]
        recv[own * 2, c] = main
        send[1, c] = jnp.where(u_me == 1, main.astype(F32), stage[c]).astype(BF16)

    for load in loads[2:]:
        load.wait()
    first = own * share

    def picked(values, at):
        lane = lax.broadcasted_iota(jnp.int32, values.shape, 1)
        return jnp.sum(jnp.where(lane == at, values, 0).astype(F32), axis=1, keepdims=True)

    row_at = lax.broadcasted_iota(jnp.int32, (width, LANES), 0)
    col_at = lax.broadcasted_iota(jnp.int32, (width, LANES), 1)
    apart = row_at - col_at
    floor_rows = []
    for k in range(share):
        win = picked(wins[...], first + k)
        floor_rows.append(jnp.broadcast_to(1e-05 * win, (1, LANES)))
        band = jnp.logical_and(apart >= 0, apart < win.astype(jnp.int32))
        bt[:, pl.ds(k * LANES, LANES)] = jnp.where(band, 1.0, 0.0).astype(BF16)
    floor_row = jnp.concatenate(floor_rows, axis=1)

    lane_at = lax.broadcasted_iota(jnp.int32, (share * GROUP, LANES), 1)

    def prepare(group):
        base = group * GROUP
        rows = lags[pl.ds(base, GROUP), :]
        lag = jnp.concatenate([picked(rows, first + k) for k in range(share)], axis=0)
        lag = jnp.broadcast_to(lag.astype(jnp.int32), (share * GROUP, LANES))
        square = (GROUP, subnet.shape[1])
        here = lax.broadcasted_iota(jnp.int32, square, 1) == base + lax.broadcasted_iota(
            jnp.int32, square, 0
        )

        def column(row):
            spread_row = jnp.broadcast_to(row.astype(F32), square)
            return jnp.sum(jnp.where(here, spread_row, 0.0), axis=1, keepdims=True)

        region = jnp.broadcast_to(column(subnet[...]).astype(jnp.int32), (GROUP, LANES))
        open_ = [column(mask[pl.ds(c, 1), :]) for c in range(CHANNELS)]
        live = jnp.maximum(functools.reduce(jnp.add, open_), 1.0)
        return lag, region, [o / live for o in open_]

    ready = prepare(0) if n_groups == 1 else None

    pl.semaphore_wait(barrier, everyone - 1)

    def outgoing(i):
        d = i + 1
        half = d % 2
        return pltpu.make_async_remote_copy(
            src_ref=send.at[half],
            dst_ref=recv.at[own * 2 + half],
            send_sem=send_sem,
            recv_sem=recv_sem,
            device_id=place(d),
            device_id_type=pl.DeviceIdType.MESH,
        )

    blocks = recv.at[pl.ds(0, everyone - 1)]
    arrived = pltpu.make_async_copy(blocks, blocks, recv_sem)
    left = pltpu.make_async_copy(blocks, blocks, send_sem)

    order = sorted(range(everyone - 1), key=lambda i: abs(i + 1 - n_own))
    if n_groups == 1:
        for i in order:
            outgoing(i).start()
    else:
        each(everyone - 1, lambda i: outgoing(i).start())

    mirror = lax.broadcasted_iota(jnp.int32, (width, width), 0) + lax.broadcasted_iota(
        jnp.int32, (width, width), 1
    )
    mirror = jnp.where(mirror == span - 1, 1.0, 0.0).astype(BF16)
    k_dev = templates.shape[1]
    for c in range(CHANNELS):
        tpad[c, :, pl.ds(0, span)] = templates[c].astype(F32)
    mirrored = jnp.dot(
        jnp.concatenate([tpad[c] for c in range(CHANNELS)], axis=0).astype(BF16),
        mirror,
        preferred_element_type=F32,
    )
    norm_rows = []
    for c in range(CHANNELS):
        norms = []
        for k in range(share):
            taps = tpad[c, pl.ds(a_me * share + k, 1), :]
            power = jnp.sum(taps * taps, axis=1, keepdims=True)
            norms.append(jnp.broadcast_to(1.0 / jnp.sqrt(power + 1e-06), (1, LANES)))
        norm_rows.append(jnp.concatenate(norms, axis=1))
        for j in range(k_blocks):
            turned = pltpu.roll(
                mirrored[c * k_dev : (c + 1) * k_dev], (j * LANES - span + 1) % width, 1
            )
            lines[c, j] = jnp.concatenate([turned[:, :LANES], turned[:, width - LANES :]], axis=1)
            for k in range(share):
                line = lines[c, j, pl.ds(a_me * share + k, 1), :]
                slid = pltpu.roll(
                    jnp.broadcast_to(line, (LANES, 2 * LANES)), 0, 1, stride=1, stride_axis=0
                )
                wt[c, pl.ds(j * LANES, LANES), pl.ds(k * LANES, LANES)] = slid[:, :LANES].astype(BF16)

    def work(group, ready):
        lag, region, weight = ready
        for o in range(owners):
            for half in range(2):
                for c in range(CHANNELS):
                    block = recv[(group * owners + o) * 2 + half, c].astype(F32)
                    for n in range(own_blocks):
                        ebuf[c, half * own_blocks + n, pl.ds(o * st_dev, st_dev), :] = block[
                            :, n * LANES : (n + 1) * LANES
                        ]

        def spread(parts):
            empty = jnp.zeros_like(parts[0])
            parts = parts + [empty] * (u_blocks + k_blocks - 1 - len(parts))
            return jnp.concatenate(
                [jnp.concatenate(parts[j : j + u_blocks], axis=0) for j in range(k_blocks)], axis=1
            )

        corr = []
        squares = []
        for c in range(CHANNELS):
            wave = [ebuf[c, n] for n in range(2 * own_blocks)]
            corr.append(
                jnp.dot(spread([w.astype(BF16) for w in wave]), wt[c], preferred_element_type=F32)
            )
            high = [(w * w).astype(BF16) for w in wave]
            low = [(w * w - h.astype(F32)).astype(BF16) for w, h in zip(wave, high)]
            squares.append(spread(high))
            squares.append(spread(low))
        energy = jnp.dot(
            jnp.concatenate(squares, axis=0), bt[...], preferred_element_type=F32
        )
        tall = u_blocks * GROUP
        coherent = None
        for c in range(CHANNELS):
            at = 2 * c * tall
            power = energy[at : at + tall] + energy[at + tall : at + 2 * tall]
            scale = jnp.concatenate([weight[c]] * u_blocks, axis=0)
            term = corr[c] * lax.rsqrt(power + floor_row) * (scale * norm_rows[c])
            coherent = term if coherent is None else coherent + term

        pieces = [
            jnp.concatenate(
                [
                    coherent[b * GROUP : (b + 1) * GROUP, k * LANES : (k + 1) * LANES]
                    for k in range(share)
                ],
                axis=0,
            )
            for b in range(u_blocks)
        ]
        for bit in range(lag_bits):
            step = 1 << bit
            turned = [pltpu.roll(p, LANES - step, 1) for p in pieces]
            stays = lane_at < LANES - step
            taken = (lax.shift_right_logical(lag, bit) & 1) == 1
            pieces = [
                jnp.where(
                    taken, jnp.where(stays, turned[b], turned[min(b + 1, u_blocks - 1)]), pieces[b]
                )
                for b in range(u_blocks)
            ]
        for k in range(share):
            for r in range(REGIONS):
                member = region == r
                total = jnp.concatenate(
                    [
                        jnp.sum(
                            jnp.where(member, pieces[n][k * GROUP : (k + 1) * GROUP], 0.0),
                            axis=0,
                            keepdims=True,
                        )
                        for n in range(own_blocks)
                    ],
                    axis=1,
                )
                if n_groups == 1:
                    out[k, pl.ds(r, 1), :] = total
                else:
                    acc[k, pl.ds(r, 1), :] += total

    if n_groups == 1:
        arrived.wait()
        work(0, ready)
    else:
        acc[...] = jnp.zeros_like(acc)
        arrived.wait()

        def one(group, carry):
            work(group, prepare(group))
            return carry

        lax.fori_loop(0, n_groups, one, 0)
        out[...] = acc[...]
    left.wait()


def shards(traces, trace_tail, templates, win_lengths, moveouts, chan_mask, subnet):
    n_tmpl = lax.axis_size("tmpl")
    n_sta = lax.axis_size("sta")
    n_own = n_tmpl * n_sta
    st_dev, _, t_dev = traces.shape
    share = templates.shape[0] // n_sta
    span = templates.shape[2]
    width = ceil_div(LANES + span - 1, LANES) * LANES
    block = (CHANNELS, st_dev, t_dev)
    operands = (
        jnp.transpose(traces, (1, 0, 2)),
        jnp.transpose(trace_tail, (1, 0, 2)),
        jnp.transpose(templates, (1, 0, 2)),
        win_lengths.reshape(1, -1),
        moveouts.T,
        chan_mask.T,
        subnet.reshape(1, -1),
    )
    return pl.pallas_call(
        functools.partial(kernel, n_sta, n_own, share),
        out_shape=jax.ShapeDtypeStruct((share, REGIONS, t_dev), F32),
        in_specs=[pl.BlockSpec(memory_space=pltpu.HBM)] * len(operands),
        out_specs=pl.BlockSpec(memory_space=pltpu.VMEM),
        scratch_shapes=[pltpu.VMEM(x.shape, x.dtype) for x in operands[1:]]
        + [
            pltpu.VMEM(block, F32),
            pltpu.VMEM((2,) + block, BF16),
            pltpu.VMEM((2 * n_own,) + block, BF16),
            pltpu.VMEM((CHANNELS, 2 * t_dev // LANES, GROUP, LANES), F32),
            pltpu.VMEM((CHANNELS, templates.shape[0], width), F32),
            pltpu.VMEM((CHANNELS, width // LANES, templates.shape[0], 2 * LANES), F32),
            pltpu.VMEM((CHANNELS, width, share * LANES), BF16),
            pltpu.VMEM((width, share * LANES), BF16),
            pltpu.VMEM((share, REGIONS, t_dev), F32),
            pltpu.SemaphoreType.DMA((len(operands),)),
            pltpu.SemaphoreType.DMA,
            pltpu.SemaphoreType.DMA,
        ],
        compiler_params=pltpu.CompilerParams(
            collective_id=0, has_side_effects=True, vmem_limit_bytes=32 * 1024 * 1024
        ),
        name="matched_filter",
    )(*(pltpu.with_memory_space_constraint(x, pltpu.HBM) for x in operands))


def solution(mesh):
    in_specs = (
        P(("tmpl", "sta"), None, ("parts", "sub")),
        P(("tmpl", "sta"), None, "parts"),
        P("tmpl", None, None),
        P(),
        P(),
        P("parts", None),
        P(),
    )
    out_specs = P(("tmpl", "sta"), None, ("parts", "sub"))
    return jax.shard_map(shards, mesh=mesh, in_specs=in_specs, out_specs=out_specs, check_vma=False)
```

```python
import functools

import jax
import jax.numpy as jnp
from jax import lax
from jax.experimental import pallas as pl
from jax.experimental.pallas import tpu as pltpu
from jax.sharding import PartitionSpec as P

REGIONS = 2
CHANNELS = 3
LANES = 128
GROUP = 16
F32 = jnp.float32
BF16 = jnp.bfloat16


def ceil_div(a, b):
    return -(-a // b)


def each(count, body):
    if count <= 16:
        for i in range(count):
            body(i)
    else:
        lax.fori_loop(0, count, lambda i, c: (body(i), c)[1], 0)


def kernel(
    n_sta, n_own, share,
    traces_hbm, tail_hbm, templates_hbm, wins_hbm, lags_hbm, mask_hbm, subnet_hbm,
    out,
    traces, tail, templates, wins, lags, mask, subnet,
    stage, send, recv, whole, tpad, lines, wt, bt, acc, load_sem, send_sem, recv_sem,
):
    _, st_dev, t_dev = traces_hbm.shape
    halo = tail.shape[2]
    span = templates.shape[2]
    lag_bits = (halo - span).bit_length()
    own_blocks = t_dev // LANES
    u_blocks = ceil_div(t_dev + halo - span + 1, LANES)
    k_blocks = ceil_div(LANES + span - 1, LANES)
    width = k_blocks * LANES
    owners = GROUP // st_dev
    n_groups = n_own // owners
    everyone = 2 * n_own

    t_me = lax.axis_index("tmpl")
    a_me = lax.axis_index("sta")
    u_me = lax.axis_index("sub")
    own = t_me * n_sta + a_me

    def place(d):
        if isinstance(d, int):
            d_t, d_a, d_u = d // (2 * n_sta), d // 2 % n_sta, d % 2
        else:
            d_t, d_a, d_u = lax.div(d, 2 * n_sta), lax.rem(lax.div(d, 2), n_sta), lax.rem(d, 2)
        return {
            "tmpl": lax.rem(t_me + d_t, n_own // n_sta),
            "sta": lax.rem(a_me + d_a, n_sta),
            "sub": lax.rem(u_me + d_u, 2),
        }

    pairs = [
        (traces_hbm, traces), (tail_hbm, tail), (templates_hbm, templates), (wins_hbm, wins),
        (lags_hbm, lags), (mask_hbm, mask), (subnet_hbm, subnet),
    ]
    loads = [pltpu.make_async_copy(a, b, load_sem.at[i]) for i, (a, b) in enumerate(pairs)]
    for load in loads:
        load.start()

    barrier = pltpu.get_barrier_semaphore()

    def greet(i):
        pl.semaphore_signal(barrier, inc=1, device_id=place(i + 1), device_id_type=pl.DeviceIdType.MESH)

    each(everyone - 1, greet)

    stage[...] = jnp.zeros_like(stage)
    tpad[...] = jnp.zeros_like(tpad)
    loads[0].wait()
    loads[1].wait()
    for c in range(CHANNELS):
        stage[c, :, pl.ds(0, halo)] = tail[c].astype(F32)
        for n in range(own_blocks):
            lanes = pl.ds(n * LANES, LANES)
            main = traces[c, :, lanes]
            send[0, n, c] = main
            send[1, n, c] = jnp.where(u_me == 1, main.astype(F32), stage[c, :, lanes]).astype(BF16)
    pltpu.make_async_copy(send.at[0], recv.at[pl.ds(0, own_blocks), :, own], recv_sem).start()

    for load in loads[2:]:
        load.wait()
    first = own * share

    def picked(values, at):
        lane = lax.broadcasted_iota(jnp.int32, values.shape, 1)
        return jnp.sum(jnp.where(lane == at, values, 0).astype(F32), axis=1, keepdims=True)

    row_at = lax.broadcasted_iota(jnp.int32, (width, LANES), 0)
    col_at = lax.broadcasted_iota(jnp.int32, (width, LANES), 1)
    apart = row_at - col_at
    floor_rows = []
    for k in range(share):
        win = picked(wins[...], first + k)
        floor_rows.append(jnp.broadcast_to(1e-05 * win, (1, LANES)))
        band = jnp.logical_and(apart >= 0, apart < win.astype(jnp.int32))
        bt[:, pl.ds(k * LANES, LANES)] = jnp.where(band, 1.0, 0.0).astype(BF16)
    floor_row = jnp.concatenate(floor_rows, axis=1)

    lane_at = lax.broadcasted_iota(jnp.int32, (share * GROUP, LANES), 1)

    def prepare(group):
        base = group * GROUP
        rows = lags[pl.ds(base, GROUP), :]
        lag = jnp.concatenate([picked(rows, first + k) for k in range(share)], axis=0)
        lag = jnp.broadcast_to(lag.astype(jnp.int32), (share * GROUP, LANES))
        square = (GROUP, subnet.shape[1])
        here = lax.broadcasted_iota(jnp.int32, square, 1) == base + lax.broadcasted_iota(
            jnp.int32, square, 0
        )

        def column(row):
            spread_row = jnp.broadcast_to(row.astype(F32), square)
            return jnp.sum(jnp.where(here, spread_row, 0.0), axis=1, keepdims=True)

        region = jnp.broadcast_to(column(subnet[...]).astype(jnp.int32), (GROUP, LANES))
        open_ = [column(mask[pl.ds(c, 1), :]) for c in range(CHANNELS)]
        live = jnp.maximum(functools.reduce(jnp.add, open_), 1.0)
        return lag, region, [o / live for o in open_]

    ready = prepare(0) if n_groups == 1 else None

    pl.semaphore_wait(barrier, everyone - 1)

    def outgoing(i):
        d = i + 1
        half = d % 2
        return pltpu.make_async_remote_copy(
            src_ref=send.at[half],
            dst_ref=recv.at[pl.ds(half * own_blocks, own_blocks), :, own],
            send_sem=send_sem,
            recv_sem=recv_sem,
            device_id=place(d),
            device_id_type=pl.DeviceIdType.MESH,
        )

    arrived = pltpu.make_async_copy(recv, recv, recv_sem)
    left = pltpu.make_async_copy(whole, whole, send_sem)

    order = sorted(range(everyone - 1), key=lambda i: abs(i + 1 - n_own))
    if n_groups == 1:
        for i in order:
            outgoing(i).start()
    else:
        each(everyone - 1, lambda i: outgoing(i).start())

    mirror = lax.broadcasted_iota(jnp.int32, (width, width), 0) + lax.broadcasted_iota(
        jnp.int32, (width, width), 1
    )
    mirror = jnp.where(mirror == span - 1, 1.0, 0.0).astype(BF16)
    k_dev = templates.shape[1]
    for c in range(CHANNELS):
        tpad[c, :, pl.ds(0, span)] = templates[c].astype(F32)
    mirrored = jnp.dot(
        jnp.concatenate([tpad[c] for c in range(CHANNELS)], axis=0).astype(BF16),
        mirror,
        preferred_element_type=F32,
    )
    norm_rows = []
    for c in range(CHANNELS):
        norms = []
        for k in range(share):
            taps = tpad[c, pl.ds(a_me * share + k, 1), :]
            power = jnp.sum(taps * taps, axis=1, keepdims=True)
            norms.append(jnp.broadcast_to(1.0 / jnp.sqrt(power + 1e-06), (1, LANES)))
        norm_rows.append(jnp.concatenate(norms, axis=1))
        for j in range(k_blocks):
            turned = pltpu.roll(
                mirrored[c * k_dev : (c + 1) * k_dev], (j * LANES - span + 1) % width, 1
            )
            lines[c, j] = jnp.concatenate([turned[:, :LANES], turned[:, width - LANES :]], axis=1)
            for k in range(share):
                line = lines[c, j, pl.ds(a_me * share + k, 1), :]
                slid = pltpu.roll(
                    jnp.broadcast_to(line, (LANES, 2 * LANES)), 0, 1, stride=1, stride_axis=0
                )
                wt[c, pl.ds(j * LANES, LANES), pl.ds(k * LANES, LANES)] = slid[:, :LANES].astype(BF16)

    def work(group, ready):
        lag, region, weight = ready
        stations = recv.reshape(2 * own_blocks, CHANNELS, n_own * st_dev, LANES)
        rows = pl.ds(group * GROUP, GROUP)

        def spread(parts):
            empty = jnp.zeros_like(parts[0])
            parts = parts + [empty] * (u_blocks + k_blocks - 1 - len(parts))
            return jnp.concatenate(
                [jnp.concatenate(parts[j : j + u_blocks], axis=0) for j in range(k_blocks)], axis=1
            )

        corr = []
        squares = []
        for c in range(CHANNELS):
            wave = [stations[n, c, rows, :] for n in range(2 * own_blocks)]
            corr.append(
                jnp.dot(spread(wave), wt[c], preferred_element_type=F32)
            )
            wave = [w.astype(F32) for w in wave]
            high = [(w * w).astype(BF16) for w in wave]
            low = [(w * w - h.astype(F32)).astype(BF16) for w, h in zip(wave, high)]
            squares.append(spread(high))
            squares.append(spread(low))
        energy = jnp.dot(
            jnp.concatenate(squares, axis=0), bt[...], preferred_element_type=F32
        )
        tall = u_blocks * GROUP
        coherent = None
        for c in range(CHANNELS):
            at = 2 * c * tall
            power = energy[at : at + tall] + energy[at + tall : at + 2 * tall]
            scale = jnp.concatenate([weight[c]] * u_blocks, axis=0)
            term = corr[c] * lax.rsqrt(power + floor_row) * (scale * norm_rows[c])
            coherent = term if coherent is None else coherent + term

        pieces = [
            jnp.concatenate(
                [
                    coherent[b * GROUP : (b + 1) * GROUP, k * LANES : (k + 1) * LANES]
                    for k in range(share)
                ],
                axis=0,
            )
            for b in range(u_blocks)
        ]
        for bit in range(lag_bits):
            step = 1 << bit
            turned = [pltpu.roll(p, LANES - step, 1) for p in pieces]
            stays = lane_at < LANES - step
            taken = (lax.shift_right_logical(lag, bit) & 1) == 1
            pieces = [
                jnp.where(
                    taken, jnp.where(stays, turned[b], turned[min(b + 1, u_blocks - 1)]), pieces[b]
                )
                for b in range(u_blocks)
            ]
        for k in range(share):
            for r in range(REGIONS):
                member = region == r
                total = jnp.concatenate(
                    [
                        jnp.sum(
                            jnp.where(member, pieces[n][k * GROUP : (k + 1) * GROUP], 0.0),
                            axis=0,
                            keepdims=True,
                        )
                        for n in range(own_blocks)
                    ],
                    axis=1,
                )
                if n_groups == 1:
                    out[k, pl.ds(r, 1), :] = total
                else:
                    acc[k, pl.ds(r, 1), :] += total

    if n_groups == 1:
        arrived.wait()
        work(0, ready)
    else:
        acc[...] = jnp.zeros_like(acc)
        arrived.wait()

        def one(group, carry):
            work(group, prepare(group))
            return carry

        lax.fori_loop(0, n_groups, one, 0)
        out[...] = acc[...]
    left.wait()


def shards(traces, trace_tail, templates, win_lengths, moveouts, chan_mask, subnet):
    n_tmpl = lax.axis_size("tmpl")
    n_sta = lax.axis_size("sta")
    n_own = n_tmpl * n_sta
    st_dev, _, t_dev = traces.shape
    share = templates.shape[0] // n_sta
    span = templates.shape[2]
    width = ceil_div(LANES + span - 1, LANES) * LANES
    blocks = t_dev // LANES
    operands = (
        jnp.transpose(traces, (1, 0, 2)),
        jnp.transpose(trace_tail, (1, 0, 2)),
        jnp.transpose(templates, (1, 0, 2)),
        win_lengths.reshape(1, -1),
        moveouts.T,
        chan_mask.T,
        subnet.reshape(1, -1),
    )
    return pl.pallas_call(
        functools.partial(kernel, n_sta, n_own, share),
        out_shape=jax.ShapeDtypeStruct((share, REGIONS, t_dev), F32),
        in_specs=[pl.BlockSpec(memory_space=pltpu.HBM)] * len(operands),
        out_specs=pl.BlockSpec(memory_space=pltpu.VMEM),
        scratch_shapes=[pltpu.VMEM(x.shape, x.dtype) for x in operands]
        + [
            pltpu.VMEM((CHANNELS, st_dev, t_dev), F32),
            pltpu.VMEM((2, blocks, CHANNELS, st_dev, LANES), BF16),
            pltpu.VMEM((2 * blocks, CHANNELS, n_own, st_dev, LANES), BF16),
            pltpu.VMEM((2 * n_own - 1, blocks, CHANNELS, st_dev, LANES), BF16),
            pltpu.VMEM((CHANNELS, templates.shape[0], width), F32),
            pltpu.VMEM((CHANNELS, width // LANES, templates.shape[0], 2 * LANES), F32),
            pltpu.VMEM((CHANNELS, width, share * LANES), BF16),
            pltpu.VMEM((width, share * LANES), BF16),
            pltpu.VMEM((share, REGIONS, t_dev), F32),
            pltpu.SemaphoreType.DMA((len(operands),)),
            pltpu.SemaphoreType.DMA,
            pltpu.SemaphoreType.DMA,
        ],
        compiler_params=pltpu.CompilerParams(
            collective_id=0, has_side_effects=True, vmem_limit_bytes=32 * 1024 * 1024
        ),
        name="matched_filter",
    )(*(pltpu.with_memory_space_constraint(x, pltpu.HBM) for x in operands))


def solution(mesh):
    in_specs = (
        P(("tmpl", "sta"), None, ("parts", "sub")),
        P(("tmpl", "sta"), None, "parts"),
        P("tmpl", None, None),
        P(),
        P(),
        P("parts", None),
        P(),
    )
    out_specs = P(("tmpl", "sta"), None, ("parts", "sub"))
    return jax.shard_map(shards, mesh=mesh, in_specs=in_specs, out_specs=out_specs, check_vma=False)
```

```python
import functools

import jax
import jax.numpy as jnp
from jax import lax
from jax.experimental import pallas as pl
from jax.experimental.pallas import tpu as pltpu
from jax.sharding import PartitionSpec as P

REGIONS = 2
CHANNELS = 3
LANES = 128
GROUP = 16
F32 = jnp.float32
BF16 = jnp.bfloat16
NT_DIMS = (((1,), (1,)), ((), ()))


def ceil_div(a, b):
    return -(-a // b)


def each(count, body):
    if count <= 16:
        for i in range(count):
            body(i)
    else:
        lax.fori_loop(0, count, lambda i, c: (body(i), c)[1], 0)


def kernel(
    n_sta, n_own, share,
    traces_hbm, tail_hbm, templates_hbm, wins_hbm, lags_hbm, mask_hbm, subnet_hbm,
    out,
    traces, tail, templates, wins, lags, mask, subnet,
    stage, send, recv, whole, tpad, wt, bt, acc, load_sem, send_sem, recv_sem,
):
    _, st_dev, t_dev = traces_hbm.shape
    halo = tail.shape[2]
    span = templates.shape[2]
    lag_bits = (halo - span).bit_length()
    own_blocks = t_dev // LANES
    u_blocks = ceil_div(t_dev + halo - span + 1, LANES)
    k_blocks = ceil_div(LANES + span - 1, LANES)
    width = k_blocks * LANES
    owners = GROUP // st_dev
    n_groups = n_own // owners
    everyone = 2 * n_own

    t_me = lax.axis_index("tmpl")
    a_me = lax.axis_index("sta")
    u_me = lax.axis_index("sub")
    own = t_me * n_sta + a_me

    def place(d):
        if isinstance(d, int):
            d_t, d_a, d_u = d // (2 * n_sta), d // 2 % n_sta, d % 2
        else:
            d_t, d_a, d_u = lax.div(d, 2 * n_sta), lax.rem(lax.div(d, 2), n_sta), lax.rem(d, 2)
        return {
            "tmpl": lax.rem(t_me + d_t, n_own // n_sta),
            "sta": lax.rem(a_me + d_a, n_sta),
            "sub": lax.rem(u_me + d_u, 2),
        }

    pairs = [
        (traces_hbm, traces), (tail_hbm, tail), (templates_hbm, templates), (wins_hbm, wins),
        (lags_hbm, lags), (mask_hbm, mask), (subnet_hbm, subnet),
    ]
    loads = [pltpu.make_async_copy(a, b, load_sem.at[i]) for i, (a, b) in enumerate(pairs)]
    for load in loads:
        load.start()

    barrier = pltpu.get_barrier_semaphore()

    def greet(i):
        pl.semaphore_signal(barrier, inc=1, device_id=place(i + 1), device_id_type=pl.DeviceIdType.MESH)

    each(everyone - 1, greet)

    stage[...] = jnp.zeros_like(stage)
    tpad[...] = jnp.zeros_like(tpad)
    loads[0].wait()
    loads[1].wait()
    for c in range(CHANNELS):
        stage[c, :, pl.ds(0, halo)] = tail[c].astype(F32)
        for n in range(own_blocks):
            lanes = pl.ds(n * LANES, LANES)
            main = traces[c, :, lanes]
            send[0, n, c] = main
            send[1, n, c] = jnp.where(u_me == 1, main.astype(F32), stage[c, :, lanes]).astype(BF16)
    pltpu.make_async_copy(send.at[0], recv.at[pl.ds(0, own_blocks), :, own], recv_sem).start()

    for load in loads[2:]:
        load.wait()
    first = own * share

    def picked(values, at):
        lane = lax.broadcasted_iota(jnp.int32, values.shape, 1)
        return jnp.sum(jnp.where(lane == at, values, 0).astype(F32), axis=1, keepdims=True)

    row_at = lax.broadcasted_iota(jnp.int32, (LANES, width), 0)
    col_at = lax.broadcasted_iota(jnp.int32, (LANES, width), 1)
    apart = col_at - row_at
    floor_rows = []
    for k in range(share):
        win = picked(wins[...], first + k)
        floor_rows.append(jnp.broadcast_to(1e-05 * win, (1, LANES)))
        band = jnp.logical_and(apart >= 0, apart < win.astype(jnp.int32))
        bt[pl.ds(k * LANES, LANES), :] = jnp.where(band, 1.0, 0.0).astype(BF16)
    floor_row = jnp.concatenate(floor_rows, axis=1)

    lane_at = lax.broadcasted_iota(jnp.int32, (share * GROUP, LANES), 1)

    def prepare(group):
        base = group * GROUP
        rows = lags[pl.ds(base, GROUP), :]
        lag = jnp.concatenate([picked(rows, first + k) for k in range(share)], axis=0)
        lag = jnp.broadcast_to(lag.astype(jnp.int32), (share * GROUP, LANES))
        square = (GROUP, subnet.shape[1])
        here = lax.broadcasted_iota(jnp.int32, square, 1) == base + lax.broadcasted_iota(
            jnp.int32, square, 0
        )

        def column(row):
            spread_row = jnp.broadcast_to(row.astype(F32), square)
            return jnp.sum(jnp.where(here, spread_row, 0.0), axis=1, keepdims=True)

        region = jnp.broadcast_to(column(subnet[...]).astype(jnp.int32), (GROUP, LANES))
        open_ = [column(mask[pl.ds(c, 1), :]) for c in range(CHANNELS)]
        live = jnp.maximum(functools.reduce(jnp.add, open_), 1.0)
        return lag, region, [o / live for o in open_]

    ready = prepare(0) if n_groups == 1 else None

    pl.semaphore_wait(barrier, everyone - 1)

    def outgoing(i):
        d = i + 1
        half = d % 2
        return pltpu.make_async_remote_copy(
            src_ref=send.at[half],
            dst_ref=recv.at[pl.ds(half * own_blocks, own_blocks), :, own],
            send_sem=send_sem,
            recv_sem=recv_sem,
            device_id=place(d),
            device_id_type=pl.DeviceIdType.MESH,
        )

    arrived = pltpu.make_async_copy(recv, recv, recv_sem)
    left = pltpu.make_async_copy(whole, whole, send_sem)

    order = sorted(range(everyone - 1), key=lambda i: abs(i + 1 - n_own))
    if n_groups == 1:
        for i in order:
            outgoing(i).start()
    else:
        each(everyone - 1, lambda i: outgoing(i).start())

    norm_rows = []
    for c in range(CHANNELS):
        tpad[c, :, pl.ds(0, span)] = templates[c].astype(F32)
        norms = []
        for k in range(share):
            taps = tpad[c, pl.ds(a_me * share + k, 1), :]
            power = jnp.sum(taps * taps, axis=1, keepdims=True)
            norms.append(jnp.broadcast_to(1.0 / jnp.sqrt(power + 1e-06), (1, LANES)))
            line = jnp.broadcast_to(taps, (LANES, width))
            slid = pltpu.roll(line, 0, 1, stride=1, stride_axis=0)
            wt[c, pl.ds(k * LANES, LANES), :] = slid.astype(BF16)
        norm_rows.append(jnp.concatenate(norms, axis=1))

    def work(group, ready):
        lag, region, weight = ready
        stations = recv.reshape(2 * own_blocks, CHANNELS, n_own * st_dev, LANES)
        rows = pl.ds(group * GROUP, GROUP)

        def spread(parts):
            empty = jnp.zeros_like(parts[0])
            parts = parts + [empty] * (u_blocks + k_blocks - 1 - len(parts))
            return jnp.concatenate(
                [jnp.concatenate(parts[j : j + u_blocks], axis=0) for j in range(k_blocks)], axis=1
            )

        corr = []
        squares = []
        for c in range(CHANNELS):
            wave = [stations[n, c, rows, :] for n in range(2 * own_blocks)]
            corr.append(
                lax.dot_general(spread(wave), wt[c], NT_DIMS, preferred_element_type=F32)
            )
            wave = [w.astype(F32) for w in wave]
            high = [(w * w).astype(BF16) for w in wave]
            low = [(w * w - h.astype(F32)).astype(BF16) for w, h in zip(wave, high)]
            squares.append(spread(high))
            squares.append(spread(low))
        energy = lax.dot_general(
            jnp.concatenate(squares, axis=0), bt[...], NT_DIMS, preferred_element_type=F32
        )
        tall = u_blocks * GROUP
        coherent = None
        for c in range(CHANNELS):
            at = 2 * c * tall
            power = energy[at : at + tall] + energy[at + tall : at + 2 * tall]
            scale = jnp.concatenate([weight[c]] * u_blocks, axis=0)
            term = corr[c] * lax.rsqrt(power + floor_row) * (scale * norm_rows[c])
            coherent = term if coherent is None else coherent + term

        pieces = [
            jnp.concatenate(
                [
                    coherent[b * GROUP : (b + 1) * GROUP, k * LANES : (k + 1) * LANES]
                    for k in range(share)
                ],
                axis=0,
            )
            for b in range(u_blocks)
        ]
        for bit in range(lag_bits):
            step = 1 << bit
            turned = [pltpu.roll(p, LANES - step, 1) for p in pieces]
            stays = lane_at < LANES - step
            taken = (lax.shift_right_logical(lag, bit) & 1) == 1
            pieces = [
                jnp.where(
                    taken, jnp.where(stays, turned[b], turned[min(b + 1, u_blocks - 1)]), pieces[b]
                )
                for b in range(u_blocks)
            ]
        for k in range(share):
            for r in range(REGIONS):
                member = region == r
                total = jnp.concatenate(
                    [
                        jnp.sum(
                            jnp.where(member, pieces[n][k * GROUP : (k + 1) * GROUP], 0.0),
                            axis=0,
                            keepdims=True,
                        )
                        for n in range(own_blocks)
                    ],
                    axis=1,
                )
                if n_groups == 1:
                    out[k, pl.ds(r, 1), :] = total
                else:
                    acc[k, pl.ds(r, 1), :] += total

    if n_groups == 1:
        arrived.wait()
        work(0, ready)
    else:
        acc[...] = jnp.zeros_like(acc)
        arrived.wait()

        def one(group, carry):
            work(group, prepare(group))
            return carry

        lax.fori_loop(0, n_groups, one, 0)
        out[...] = acc[...]
    left.wait()


def shards(traces, trace_tail, templates, win_lengths, moveouts, chan_mask, subnet):
    n_tmpl = lax.axis_size("tmpl")
    n_sta = lax.axis_size("sta")
    n_own = n_tmpl * n_sta
    st_dev, _, t_dev = traces.shape
    share = templates.shape[0] // n_sta
    span = templates.shape[2]
    width = ceil_div(LANES + span - 1, LANES) * LANES
    blocks = t_dev // LANES
    operands = (
        jnp.transpose(traces, (1, 0, 2)),
        jnp.transpose(trace_tail, (1, 0, 2)),
        jnp.transpose(templates, (1, 0, 2)),
        win_lengths.reshape(1, -1),
        moveouts.T,
        chan_mask.T,
        subnet.reshape(1, -1),
    )
    return pl.pallas_call(
        functools.partial(kernel, n_sta, n_own, share),
        out_shape=jax.ShapeDtypeStruct((share, REGIONS, t_dev), F32),
        in_specs=[pl.BlockSpec(memory_space=pltpu.HBM)] * len(operands),
        out_specs=pl.BlockSpec(memory_space=pltpu.VMEM),
        scratch_shapes=[pltpu.VMEM(x.shape, x.dtype) for x in operands]
        + [
            pltpu.VMEM((CHANNELS, st_dev, t_dev), F32),
            pltpu.VMEM((2, blocks, CHANNELS, st_dev, LANES), BF16),
            pltpu.VMEM((2 * blocks, CHANNELS, n_own, st_dev, LANES), BF16),
            pltpu.VMEM((2 * n_own - 1, blocks, CHANNELS, st_dev, LANES), BF16),
            pltpu.VMEM((CHANNELS, templates.shape[0], width), F32),
            pltpu.VMEM((CHANNELS, share * LANES, width), BF16),
            pltpu.VMEM((share * LANES, width), BF16),
            pltpu.VMEM((share, REGIONS, t_dev), F32),
            pltpu.SemaphoreType.DMA((len(operands),)),
            pltpu.SemaphoreType.DMA,
            pltpu.SemaphoreType.DMA,
        ],
        compiler_params=pltpu.CompilerParams(
            collective_id=0, has_side_effects=True, vmem_limit_bytes=32 * 1024 * 1024
        ),
        name="matched_filter",
    )(*(pltpu.with_memory_space_constraint(x, pltpu.HBM) for x in operands))


def solution(mesh):
    in_specs = (
        P(("tmpl", "sta"), None, ("parts", "sub")),
        P(("tmpl", "sta"), None, "parts"),
        P("tmpl", None, None),
        P(),
        P(),
        P("parts", None),
        P(),
    )
    out_specs = P(("tmpl", "sta"), None, ("parts", "sub"))
    return jax.shard_map(shards, mesh=mesh, in_specs=in_specs, out_specs=out_specs, check_vma=False)
```

```python
import functools

import jax
import jax.numpy as jnp
from jax import lax
from jax.experimental import pallas as pl
from jax.experimental.pallas import tpu as pltpu
from jax.sharding import PartitionSpec as P

REGIONS = 2
CHANNELS = 3
LANES = 128
GROUP = 16
PAIR = 2
F32 = jnp.float32
BF16 = jnp.bfloat16


def ceil_div(a, b):
    return -(-a // b)


def each(count, body):
    if count <= 16:
        for i in range(count):
            body(i)
    else:
        lax.fori_loop(0, count, lambda i, c: (body(i), c)[1], 0)


def kernel(
    n_sta, n_own, share,
    traces_hbm, tail_hbm, templates_hbm, wins_hbm, lags_hbm, mask_hbm, subnet_hbm,
    out,
    tail, templates, wins, lags, mask, subnet,
    stage, send, recv, ebuf, tpad, lines, wt, bt, acc, load_sem, send_sem, recv_sem,
):
    _, st_dev, t_dev = traces_hbm.shape
    halo = tail.shape[2]
    span = templates.shape[2]
    lag_bits = (halo - span).bit_length()
    own_blocks = t_dev // LANES
    u_blocks = ceil_div(t_dev + halo - span + 1, LANES)
    k_blocks = ceil_div(LANES + span - 1, LANES)
    width = k_blocks * LANES
    owners = GROUP // st_dev
    n_groups = n_own // owners
    everyone = 2 * n_own

    t_me = lax.axis_index("tmpl")
    a_me = lax.axis_index("sta")
    u_me = lax.axis_index("sub")
    own = t_me * n_sta + a_me

    def place(d):
        if isinstance(d, int):
            d_t, d_a, d_u = d // (2 * n_sta), d // 2 % n_sta, d % 2
        else:
            d_t, d_a, d_u = lax.div(d, 2 * n_sta), lax.rem(lax.div(d, 2), n_sta), lax.rem(d, 2)
        return {
            "tmpl": lax.rem(t_me + d_t, n_own // n_sta),
            "sta": lax.rem(a_me + d_a, n_sta),
            "sub": lax.rem(u_me + d_u, 2),
        }

    pairs = [
        (traces_hbm, send.at[0]), (tail_hbm, tail), (templates_hbm, templates), (wins_hbm, wins),
        (lags_hbm, lags), (mask_hbm, mask), (subnet_hbm, subnet),
    ]
    loads = [pltpu.make_async_copy(a, b, load_sem.at[i]) for i, (a, b) in enumerate(pairs)]
    for load in loads:
        load.start()

    barrier = pltpu.get_barrier_semaphore()

    def greet(i):
        pl.semaphore_signal(barrier, inc=1, device_id=place(i + 1), device_id_type=pl.DeviceIdType.MESH)

    each(everyone - 1, greet)

    stage[...] = jnp.zeros_like(stage)
    tpad[...] = jnp.zeros_like(tpad)
    loads[0].wait()
    loads[1].wait()
    for c in range(CHANNELS):
        stage[c, :, pl.ds(0, halo)] = tail[c].astype(F32)
        main = send[0, c]
        recv[own * 2, c] = main
        send[1, c] = jnp.where(u_me == 1, main.astype(F32), stage[c]).astype(BF16)

    for load in loads[2:]:
        load.wait()
    first = own * share

    def picked(values, at):
        lane = lax.broadcasted_iota(jnp.int32, values.shape, 1)
        return jnp.sum(jnp.where(lane == at, values, 0).astype(F32), axis=1, keepdims=True)

    row_at = lax.broadcasted_iota(jnp.int32, (width, LANES), 0)
    col_at = lax.broadcasted_iota(jnp.int32, (width, LANES), 1)
    apart = row_at - col_at
    floor_rows = []
    for k in range(share):
        win = picked(wins[...], first + k)
        floor_rows.append(jnp.broadcast_to(1e-05 * win, (1, LANES)))
        band = jnp.logical_and(apart >= 0, apart < win.astype(jnp.int32))
        bt[:, pl.ds(k * LANES, LANES)] = jnp.where(band, 1.0, 0.0).astype(BF16)
    floor_row = jnp.concatenate(floor_rows, axis=1)

    lane_at = lax.broadcasted_iota(jnp.int32, (share * GROUP, LANES), 1)

    def prepare(group):
        base = group * GROUP
        rows = lags[pl.ds(base, GROUP), :]
        lag = jnp.concatenate([picked(rows, first + k) for k in range(share)], axis=0)
        lag = jnp.broadcast_to(lag.astype(jnp.int32), (share * GROUP, LANES))
        square = (GROUP, subnet.shape[1])
        here = lax.broadcasted_iota(jnp.int32, square, 1) == base + lax.broadcasted_iota(
            jnp.int32, square, 0
        )

        def column(row):
            spread_row = jnp.broadcast_to(row.astype(F32), square)
            return jnp.sum(jnp.where(here, spread_row, 0.0), axis=1, keepdims=True)

        region = jnp.broadcast_to(column(subnet[...]).astype(jnp.int32), (GROUP, LANES))
        open_ = [column(mask[pl.ds(c, 1), :]) for c in range(CHANNELS)]
        live = jnp.maximum(functools.reduce(jnp.add, open_), 1.0)
        return lag, region, [o / live for o in open_]

    ready = prepare(0) if n_groups == 1 else None

    pl.semaphore_wait(barrier, everyone - 1)

    def outgoing(i):
        d = i + 1
        half = d % 2
        return pltpu.make_async_remote_copy(
            src_ref=send.at[half],
            dst_ref=recv.at[own * 2 + half],
            send_sem=send_sem,
            recv_sem=recv_sem,
            device_id=place(d),
            device_id_type=pl.DeviceIdType.MESH,
        )

    blocks = recv.at[pl.ds(0, everyone - 1)]
    arrived = pltpu.make_async_copy(blocks, blocks, recv_sem)
    left = pltpu.make_async_copy(blocks, blocks, send_sem)

    order = sorted(range(everyone - 1), key=lambda i: abs(i + 1 - n_own))
    if n_groups == 1:
        for i in order:
            outgoing(i).start()
    else:
        each(everyone - 1, lambda i: outgoing(i).start())

    mirror = lax.broadcasted_iota(jnp.int32, (width, width), 0) + lax.broadcasted_iota(
        jnp.int32, (width, width), 1
    )
    mirror = jnp.where(mirror == span - 1, 1.0, 0.0).astype(BF16)
    k_dev = templates.shape[1]
    for c in range(CHANNELS):
        tpad[c, :, pl.ds(0, span)] = templates[c].astype(F32)
    mirrored = jnp.dot(
        jnp.concatenate([tpad[c] for c in range(CHANNELS)], axis=0).astype(BF16),
        mirror,
        preferred_element_type=F32,
    )
    norm_rows = []
    for c in range(CHANNELS):
        norms = []
        for k in range(share):
            taps = tpad[c, pl.ds(a_me * share + k, 1), :]
            power = jnp.sum(taps * taps, axis=1, keepdims=True)
            norms.append(jnp.broadcast_to(1.0 / jnp.sqrt(power + 1e-06), (1, LANES)))
        norm_rows.append(jnp.concatenate(norms, axis=1))
        for j in range(k_blocks):
            turned = pltpu.roll(
                mirrored[c * k_dev : (c + 1) * k_dev], (j * LANES - span + 1) % width, 1
            )
            lines[c, j] = jnp.concatenate([turned[:, :LANES], turned[:, width - LANES :]], axis=1)
            for k in range(share):
                line = lines[c, j, pl.ds(a_me * share + k, 1), :]
                slid = pltpu.roll(
                    jnp.broadcast_to(line, (LANES, 2 * LANES)), 0, 1, stride=1, stride_axis=0
                )
                wt[c, pl.ds(j * LANES, LANES), pl.ds(k * LANES, LANES)] = slid[:, :LANES].astype(BF16)

    def work(group, ready):
        lag, region, weight = ready
        for o in range(owners):
            for half in range(2):
                for c in range(CHANNELS):
                    block = recv[(group * owners + o) * 2 + half, c].astype(F32)
                    for n in range(own_blocks):
                        ebuf[c, half * own_blocks + n, pl.ds(o * st_dev, st_dev), :] = block[
                            :, n * LANES : (n + 1) * LANES
                        ]

        def spread(parts):
            empty = jnp.zeros_like(parts[0])
            parts = parts + [empty] * (u_blocks + k_blocks - 1 - len(parts))
            return jnp.concatenate(
                [jnp.concatenate(parts[j : j + u_blocks], axis=0) for j in range(k_blocks)], axis=1
            )

        waves = []
        squares = []
        for c in range(CHANNELS):
            wave = [ebuf[c, n] for n in range(2 * own_blocks)]
            waves.append(spread([w.astype(BF16) for w in wave]))
            high = [(w * w).astype(BF16) for w in wave]
            low = [(w * w - h.astype(F32)).astype(BF16) for w, h in zip(wave, high)]
            squares.append(spread(high))
            squares.append(spread(low))
        squares = jnp.concatenate(squares, axis=0)
        tall = u_blocks * GROUP
        scales = [jnp.concatenate([weight[c]] * u_blocks, axis=0) for c in range(CHANNELS)]
        for start in range(0, share, PAIR):
            count = min(PAIR, share - start)
            picks = slice(start * LANES, (start + count) * LANES)
            energy = jnp.dot(squares, bt[:, picks], preferred_element_type=F32)
            coherent = None
            for c in range(CHANNELS):
                at = 2 * c * tall
                power = energy[at : at + tall] + energy[at + tall : at + 2 * tall]
                corr = jnp.dot(waves[c], wt[c, :, picks], preferred_element_type=F32)
                scale = scales[c] * norm_rows[c][:, picks]
                term = corr * lax.rsqrt(power + floor_row[:, picks]) * scale
                coherent = term if coherent is None else coherent + term
            tops = slice(start * GROUP, (start + count) * GROUP)
            lag_pair = lag[tops]
            lanes = lane_at[tops]
            pieces = [
                jnp.concatenate(
                    [
                        coherent[b * GROUP : (b + 1) * GROUP, k * LANES : (k + 1) * LANES]
                        for k in range(count)
                    ],
                    axis=0,
                )
                for b in range(u_blocks)
            ]
            for bit in range(lag_bits):
                step = 1 << bit
                turned = [pltpu.roll(p, LANES - step, 1) for p in pieces]
                stays = lanes < LANES - step
                taken = (lax.shift_right_logical(lag_pair, bit) & 1) == 1
                pieces = [
                    jnp.where(
                        taken,
                        jnp.where(stays, turned[b], turned[min(b + 1, u_blocks - 1)]),
                        pieces[b],
                    )
                    for b in range(u_blocks)
                ]
            for k in range(count):
                for r in range(REGIONS):
                    member = region == r
                    total = jnp.concatenate(
                        [
                            jnp.sum(
                                jnp.where(member, pieces[n][k * GROUP : (k + 1) * GROUP], 0.0),
                                axis=0,
                                keepdims=True,
                            )
                            for n in range(own_blocks)
                        ],
                        axis=1,
                    )
                    if n_groups == 1:
                        out[start + k, pl.ds(r, 1), :] = total
                    else:
                        acc[start + k, pl.ds(r, 1), :] += total

    if n_groups == 1:
        arrived.wait()
        work(0, ready)
    else:
        acc[...] = jnp.zeros_like(acc)
        arrived.wait()

        def one(group, carry):
            work(group, prepare(group))
            return carry

        lax.fori_loop(0, n_groups, one, 0)
        out[...] = acc[...]
    left.wait()


def shards(traces, trace_tail, templates, win_lengths, moveouts, chan_mask, subnet):
    n_tmpl = lax.axis_size("tmpl")
    n_sta = lax.axis_size("sta")
    n_own = n_tmpl * n_sta
    st_dev, _, t_dev = traces.shape
    share = templates.shape[0] // n_sta
    span = templates.shape[2]
    width = ceil_div(LANES + span - 1, LANES) * LANES
    block = (CHANNELS, st_dev, t_dev)
    operands = (
        jnp.transpose(traces, (1, 0, 2)),
        jnp.transpose(trace_tail, (1, 0, 2)),
        jnp.transpose(templates, (1, 0, 2)),
        win_lengths.reshape(1, -1),
        moveouts.T,
        chan_mask.T,
        subnet.reshape(1, -1),
    )
    return pl.pallas_call(
        functools.partial(kernel, n_sta, n_own, share),
        out_shape=jax.ShapeDtypeStruct((share, REGIONS, t_dev), F32),
        in_specs=[pl.BlockSpec(memory_space=pltpu.HBM)] * len(operands),
        out_specs=pl.BlockSpec(memory_space=pltpu.VMEM),
        scratch_shapes=[pltpu.VMEM(x.shape, x.dtype) for x in operands[1:]]
        + [
            pltpu.VMEM(block, F32),
            pltpu.VMEM((2,) + block, BF16),
            pltpu.VMEM((2 * n_own,) + block, BF16),
            pltpu.VMEM((CHANNELS, 2 * t_dev // LANES, GROUP, LANES), F32),
            pltpu.VMEM((CHANNELS, templates.shape[0], width), F32),
            pltpu.VMEM((CHANNELS, width // LANES, templates.shape[0], 2 * LANES), F32),
            pltpu.VMEM((CHANNELS, width, share * LANES), BF16),
            pltpu.VMEM((width, share * LANES), BF16),
            pltpu.VMEM((share, REGIONS, t_dev), F32),
            pltpu.SemaphoreType.DMA((len(operands),)),
            pltpu.SemaphoreType.DMA,
            pltpu.SemaphoreType.DMA,
        ],
        compiler_params=pltpu.CompilerParams(
            collective_id=0, has_side_effects=True, vmem_limit_bytes=32 * 1024 * 1024
        ),
        name="matched_filter",
    )(*(pltpu.with_memory_space_constraint(x, pltpu.HBM) for x in operands))


def solution(mesh):
    in_specs = (
        P(("tmpl", "sta"), None, ("parts", "sub")),
        P(("tmpl", "sta"), None, "parts"),
        P("tmpl", None, None),
        P(),
        P(),
        P("parts", None),
        P(),
    )
    out_specs = P(("tmpl", "sta"), None, ("parts", "sub"))
    return jax.shard_map(shards, mesh=mesh, in_specs=in_specs, out_specs=out_specs, check_vma=False)
```

```python
import functools

import jax
import jax.numpy as jnp
from jax import lax
from jax.experimental import pallas as pl
from jax.experimental.pallas import tpu as pltpu
from jax.sharding import PartitionSpec as P

REGIONS = 2
CHANNELS = 3
LANES = 128
GROUP = 16
PAIR = 2
F32 = jnp.float32
BF16 = jnp.bfloat16


def ceil_div(a, b):
    return -(-a // b)


def each(count, body):
    if count <= 16:
        for i in range(count):
            body(i)
    else:
        lax.fori_loop(0, count, lambda i, c: (body(i), c)[1], 0)


def kernel(
    n_sta, n_own, share,
    traces_hbm, tail_hbm, templates_hbm, wins_hbm, lags_hbm, mask_hbm, subnet_hbm,
    out,
    tail, templates, wins, lags, mask, subnet,
    stage, send, recv, ebuf, tpad, lines, wt, bt, acc, load_sem, send_sem, recv_sem,
):
    _, st_dev, t_dev = traces_hbm.shape
    halo = tail.shape[2]
    span = templates.shape[2]
    lag_bits = (halo - span).bit_length()
    own_blocks = t_dev // LANES
    u_blocks = ceil_div(t_dev + halo - span + 1, LANES)
    k_blocks = ceil_div(LANES + span - 1, LANES)
    width = k_blocks * LANES
    owners = GROUP // st_dev
    n_groups = n_own // owners
    everyone = 2 * n_own

    t_me = lax.axis_index("tmpl")
    a_me = lax.axis_index("sta")
    u_me = lax.axis_index("sub")
    own = t_me * n_sta + a_me

    def place(d):
        if isinstance(d, int):
            d_t, d_a, d_u = d // (2 * n_sta), d // 2 % n_sta, d % 2
        else:
            d_t, d_a, d_u = lax.div(d, 2 * n_sta), lax.rem(lax.div(d, 2), n_sta), lax.rem(d, 2)
        return {
            "tmpl": lax.rem(t_me + d_t, n_own // n_sta),
            "sta": lax.rem(a_me + d_a, n_sta),
            "sub": lax.rem(u_me + d_u, 2),
        }

    pairs = [
        (traces_hbm, send.at[0]), (tail_hbm, tail), (templates_hbm, templates), (wins_hbm, wins),
        (lags_hbm, lags), (mask_hbm, mask), (subnet_hbm, subnet),
    ]
    loads = [pltpu.make_async_copy(a, b, load_sem.at[i]) for i, (a, b) in enumerate(pairs)]
    barrier = pltpu.get_barrier_semaphore()

    def greet(i):
        pl.semaphore_signal(barrier, inc=1, device_id=place(i + 1), device_id_type=pl.DeviceIdType.MESH)

    order = sorted(range(everyone - 1), key=lambda i: abs(i + 1 - n_own))
    if n_groups == 1:
        for i in order:
            greet(i)
    else:
        each(everyone - 1, greet)
    for load in loads:
        load.start()

    stage[...] = jnp.zeros_like(stage)
    tpad[...] = jnp.zeros_like(tpad)
    loads[0].wait()
    loads[1].wait()
    for c in range(CHANNELS):
        stage[c, :, pl.ds(0, halo)] = tail[c].astype(F32)
        main = send[0, c]
        recv[own * 2, c] = main
        send[1, c] = jnp.where(u_me == 1, main.astype(F32), stage[c]).astype(BF16)

    pl.semaphore_wait(barrier, everyone - 1)

    def outgoing(i):
        d = i + 1
        half = d % 2
        return pltpu.make_async_remote_copy(
            src_ref=send.at[half],
            dst_ref=recv.at[own * 2 + half],
            send_sem=send_sem,
            recv_sem=recv_sem,
            device_id=place(d),
            device_id_type=pl.DeviceIdType.MESH,
        )

    blocks = recv.at[pl.ds(0, everyone - 1)]
    arrived = pltpu.make_async_copy(blocks, blocks, recv_sem)
    left = pltpu.make_async_copy(blocks, blocks, send_sem)

    if n_groups == 1:
        for i in order:
            outgoing(i).start()
    else:
        each(everyone - 1, lambda i: outgoing(i).start())

    for load in loads[2:]:
        load.wait()
    first = own * share

    def picked(values, at):
        lane = lax.broadcasted_iota(jnp.int32, values.shape, 1)
        return jnp.sum(jnp.where(lane == at, values, 0).astype(F32), axis=1, keepdims=True)

    row_at = lax.broadcasted_iota(jnp.int32, (width, LANES), 0)
    col_at = lax.broadcasted_iota(jnp.int32, (width, LANES), 1)
    apart = row_at - col_at
    floor_rows = []
    for k in range(share):
        win = picked(wins[...], first + k)
        floor_rows.append(jnp.broadcast_to(1e-05 * win, (1, LANES)))
        band = jnp.logical_and(apart >= 0, apart < win.astype(jnp.int32))
        bt[:, pl.ds(k * LANES, LANES)] = jnp.where(band, 1.0, 0.0).astype(BF16)
    floor_row = jnp.concatenate(floor_rows, axis=1)

    lane_at = lax.broadcasted_iota(jnp.int32, (share * GROUP, LANES), 1)

    def prepare(group):
        base = group * GROUP
        rows = lags[pl.ds(base, GROUP), :]
        lag = jnp.concatenate([picked(rows, first + k) for k in range(share)], axis=0)
        lag = jnp.broadcast_to(lag.astype(jnp.int32), (share * GROUP, LANES))
        square = (GROUP, subnet.shape[1])
        here = lax.broadcasted_iota(jnp.int32, square, 1) == base + lax.broadcasted_iota(
            jnp.int32, square, 0
        )

        def column(row):
            spread_row = jnp.broadcast_to(row.astype(F32), square)
            return jnp.sum(jnp.where(here, spread_row, 0.0), axis=1, keepdims=True)

        region = jnp.broadcast_to(column(subnet[...]).astype(jnp.int32), (GROUP, LANES))
        open_ = [column(mask[pl.ds(c, 1), :]) for c in range(CHANNELS)]
        live = jnp.maximum(functools.reduce(jnp.add, open_), 1.0)
        return lag, region, [o / live for o in open_]

    ready = prepare(0) if n_groups == 1 else None

    mirror = lax.broadcasted_iota(jnp.int32, (width, width), 0) + lax.broadcasted_iota(
        jnp.int32, (width, width), 1
    )
    mirror = jnp.where(mirror == span - 1, 1.0, 0.0).astype(BF16)
    k_dev = templates.shape[1]
    for c in range(CHANNELS):
        tpad[c, :, pl.ds(0, span)] = templates[c].astype(F32)
    mirrored = jnp.dot(
        jnp.concatenate([tpad[c] for c in range(CHANNELS)], axis=0).astype(BF16),
        mirror,
        preferred_element_type=F32,
    )
    norm_rows = []
    for c in range(CHANNELS):
        norms = []
        for k in range(share):
            taps = tpad[c, pl.ds(a_me * share + k, 1), :]
            power = jnp.sum(taps * taps, axis=1, keepdims=True)
            norms.append(jnp.broadcast_to(1.0 / jnp.sqrt(power + 1e-06), (1, LANES)))
        norm_rows.append(jnp.concatenate(norms, axis=1))
        for j in range(k_blocks):
            turned = pltpu.roll(
                mirrored[c * k_dev : (c + 1) * k_dev], (j * LANES - span + 1) % width, 1
            )
            lines[c, j] = jnp.concatenate([turned[:, :LANES], turned[:, width - LANES :]], axis=1)
            for k in range(share):
                line = lines[c, j, pl.ds(a_me * share + k, 1), :]
                slid = pltpu.roll(
                    jnp.broadcast_to(line, (LANES, 2 * LANES)), 0, 1, stride=1, stride_axis=0
                )
                wt[c, pl.ds(j * LANES, LANES), pl.ds(k * LANES, LANES)] = slid[:, :LANES].astype(BF16)

    def work(group, ready):
        lag, region, weight = ready
        for o in range(owners):
            for half in range(2):
                for c in range(CHANNELS):
                    block = recv[(group * owners + o) * 2 + half, c].astype(F32)
                    for n in range(own_blocks):
                        ebuf[c, half * own_blocks + n, pl.ds(o * st_dev, st_dev), :] = block[
                            :, n * LANES : (n + 1) * LANES
                        ]

        def spread(parts):
            empty = jnp.zeros_like(parts[0])
            parts = parts + [empty] * (u_blocks + k_blocks - 1 - len(parts))
            return jnp.concatenate(
                [jnp.concatenate(parts[j : j + u_blocks], axis=0) for j in range(k_blocks)], axis=1
            )

        waves = []
        squares = []
        for c in range(CHANNELS):
            wave = [ebuf[c, n] for n in range(2 * own_blocks)]
            waves.append(spread([w.astype(BF16) for w in wave]))
            high = [(w * w).astype(BF16) for w in wave]
            low = [(w * w - h.astype(F32)).astype(BF16) for w, h in zip(wave, high)]
            squares.append(spread(high))
            squares.append(spread(low))
        squares = jnp.concatenate(squares, axis=0)
        tall = u_blocks * GROUP
        scales = [jnp.concatenate([weight[c]] * u_blocks, axis=0) for c in range(CHANNELS)]
        for start in range(0, share, PAIR):
            count = min(PAIR, share - start)
            picks = slice(start * LANES, (start + count) * LANES)
            energy = jnp.dot(squares, bt[:, picks], preferred_element_type=F32)
            coherent = None
            for c in range(CHANNELS):
                at = 2 * c * tall
                power = energy[at : at + tall] + energy[at + tall : at + 2 * tall]
                corr = jnp.dot(waves[c], wt[c, :, picks], preferred_element_type=F32)
                scale = scales[c] * norm_rows[c][:, picks]
                term = corr * lax.rsqrt(power + floor_row[:, picks]) * scale
                coherent = term if coherent is None else coherent + term
            tops = slice(start * GROUP, (start + count) * GROUP)
            lag_pair = lag[tops]
            lanes = lane_at[tops]
            pieces = [
                jnp.concatenate(
                    [
                        coherent[b * GROUP : (b + 1) * GROUP, k * LANES : (k + 1) * LANES]
                        for k in range(count)
                    ],
                    axis=0,
                )
                for b in range(u_blocks)
            ]
            for bit in range(lag_bits):
                step = 1 << bit
                turned = [pltpu.roll(p, LANES - step, 1) for p in pieces]
                stays = lanes < LANES - step
                taken = (lax.shift_right_logical(lag_pair, bit) & 1) == 1
                pieces = [
                    jnp.where(
                        taken,
                        jnp.where(stays, turned[b], turned[min(b + 1, u_blocks - 1)]),
                        pieces[b],
                    )
                    for b in range(u_blocks)
                ]
            for k in range(count):
                for r in range(REGIONS):
                    member = region == r
                    total = jnp.concatenate(
                        [
                            jnp.sum(
                                jnp.where(member, pieces[n][k * GROUP : (k + 1) * GROUP], 0.0),
                                axis=0,
                                keepdims=True,
                            )
                            for n in range(own_blocks)
                        ],
                        axis=1,
                    )
                    if n_groups == 1:
                        out[start + k, pl.ds(r, 1), :] = total
                    else:
                        acc[start + k, pl.ds(r, 1), :] += total

    if n_groups == 1:
        arrived.wait()
        work(0, ready)
    else:
        acc[...] = jnp.zeros_like(acc)
        arrived.wait()

        def one(group, carry):
            work(group, prepare(group))
            return carry

        lax.fori_loop(0, n_groups, one, 0)
        out[...] = acc[...]
    left.wait()


def shards(traces, trace_tail, templates, win_lengths, moveouts, chan_mask, subnet):
    n_tmpl = lax.axis_size("tmpl")
    n_sta = lax.axis_size("sta")
    n_own = n_tmpl * n_sta
    st_dev, _, t_dev = traces.shape
    share = templates.shape[0] // n_sta
    span = templates.shape[2]
    width = ceil_div(LANES + span - 1, LANES) * LANES
    block = (CHANNELS, st_dev, t_dev)
    operands = (
        jnp.transpose(traces, (1, 0, 2)),
        jnp.transpose(trace_tail, (1, 0, 2)),
        jnp.transpose(templates, (1, 0, 2)),
        win_lengths.reshape(1, -1),
        moveouts.T,
        chan_mask.T,
        subnet.reshape(1, -1),
    )
    return pl.pallas_call(
        functools.partial(kernel, n_sta, n_own, share),
        out_shape=jax.ShapeDtypeStruct((share, REGIONS, t_dev), F32),
        in_specs=[pl.BlockSpec(memory_space=pltpu.HBM)] * len(operands),
        out_specs=pl.BlockSpec(memory_space=pltpu.VMEM),
        scratch_shapes=[pltpu.VMEM(x.shape, x.dtype) for x in operands[1:]]
        + [
            pltpu.VMEM(block, F32),
            pltpu.VMEM((2,) + block, BF16),
            pltpu.VMEM((2 * n_own,) + block, BF16),
            pltpu.VMEM((CHANNELS, 2 * t_dev // LANES, GROUP, LANES), F32),
            pltpu.VMEM((CHANNELS, templates.shape[0], width), F32),
            pltpu.VMEM((CHANNELS, width // LANES, templates.shape[0], 2 * LANES), F32),
            pltpu.VMEM((CHANNELS, width, share * LANES), BF16),
            pltpu.VMEM((width, share * LANES), BF16),
            pltpu.VMEM((share, REGIONS, t_dev), F32),
            pltpu.SemaphoreType.DMA((len(operands),)),
            pltpu.SemaphoreType.DMA,
            pltpu.SemaphoreType.DMA,
        ],
        compiler_params=pltpu.CompilerParams(
            collective_id=0, has_side_effects=True, vmem_limit_bytes=32 * 1024 * 1024
        ),
        name="matched_filter",
    )(*(pltpu.with_memory_space_constraint(x, pltpu.HBM) for x in operands))


def solution(mesh):
    in_specs = (
        P(("tmpl", "sta"), None, ("parts", "sub")),
        P(("tmpl", "sta"), None, "parts"),
        P("tmpl", None, None),
        P(),
        P(),
        P("parts", None),
        P(),
    )
    out_specs = P(("tmpl", "sta"), None, ("parts", "sub"))
    return jax.shard_map(shards, mesh=mesh, in_specs=in_specs, out_specs=out_specs, check_vma=False)
```

```python
import functools

import jax
import jax.numpy as jnp
from jax import lax
from jax.experimental import pallas as pl
from jax.experimental.pallas import tpu as pltpu
from jax.sharding import PartitionSpec as P

REGIONS = 2
CHANNELS = 3
LANES = 128
GROUP = 16
PAIR = 2
F32 = jnp.float32
BF16 = jnp.bfloat16


def ceil_div(a, b):
    return -(-a // b)


def each(count, body):
    if count <= 16:
        for i in range(count):
            body(i)
    else:
        lax.fori_loop(0, count, lambda i, c: (body(i), c)[1], 0)


def kernel(
    n_sta, n_own, share,
    traces_hbm, tail_hbm, templates_hbm, wins_hbm, lags_hbm, mask_hbm, subnet_hbm,
    out,
    tail, templates, wins, lags, mask, subnet,
    stage, send, recv, ebuf, tpad, lines, wt, bt, acc, load_sem, send_sem, recv_sem,
):
    _, st_dev, t_dev = traces_hbm.shape
    halo = tail.shape[2]
    span = templates.shape[2]
    lag_bits = (halo - span).bit_length()
    own_blocks = t_dev // LANES
    u_blocks = ceil_div(t_dev + halo - span + 1, LANES)
    k_blocks = ceil_div(LANES + span - 1, LANES)
    width = k_blocks * LANES
    owners = GROUP // st_dev
    n_groups = n_own // owners
    everyone = 2 * n_own

    t_me = lax.axis_index("tmpl")
    a_me = lax.axis_index("sta")
    u_me = lax.axis_index("sub")
    own = t_me * n_sta + a_me

    def place(d):
        if isinstance(d, int):
            d_t, d_a, d_u = d // (2 * n_sta), d // 2 % n_sta, d % 2
        else:
            d_t, d_a, d_u = lax.div(d, 2 * n_sta), lax.rem(lax.div(d, 2), n_sta), lax.rem(d, 2)
        return {
            "tmpl": lax.rem(t_me + d_t, n_own // n_sta),
            "sta": lax.rem(a_me + d_a, n_sta),
            "sub": lax.rem(u_me + d_u, 2),
        }

    pairs = [
        (traces_hbm, send.at[0]), (tail_hbm, tail), (templates_hbm, templates), (wins_hbm, wins),
        (lags_hbm, lags), (mask_hbm, mask), (subnet_hbm, subnet),
    ]
    loads = [pltpu.make_async_copy(a, b, load_sem.at[i]) for i, (a, b) in enumerate(pairs)]
    barrier = pltpu.get_barrier_semaphore()

    def greet(i):
        pl.semaphore_signal(barrier, inc=1, device_id=place(i + 1), device_id_type=pl.DeviceIdType.MESH)

    order = sorted(range(everyone - 1), key=lambda i: abs(i + 1 - n_own))
    if n_groups == 1:
        for i in order:
            greet(i)
    else:
        each(everyone - 1, greet)
    for load in loads:
        load.start()

    stage[...] = jnp.zeros_like(stage)
    tpad[...] = jnp.zeros_like(tpad)
    loads[0].wait()
    loads[1].wait()
    for c in range(CHANNELS):
        stage[c, :, pl.ds(0, halo)] = tail[c].astype(F32)
        main = send[0, c]
        recv[own * 2, c] = main
        send[1, c] = jnp.where(u_me == 1, main.astype(F32), stage[c]).astype(BF16)

    pl.semaphore_wait(barrier, everyone - 1)

    def outgoing(i):
        d = i + 1
        half = d % 2
        return pltpu.make_async_remote_copy(
            src_ref=send.at[half],
            dst_ref=recv.at[own * 2 + half],
            send_sem=send_sem,
            recv_sem=recv_sem,
            device_id=place(d),
            device_id_type=pl.DeviceIdType.MESH,
        )

    half_way = ceil_div(len(order), 2)
    mixed = [i for pair in zip(order[:half_way], order[:half_way - 1:-1]) for i in pair]
    mixed += order[half_way - 1 : half_way] if len(order) % 2 else []

    blocks = recv.at[pl.ds(0, everyone - 1)]
    arrived = pltpu.make_async_copy(blocks, blocks, recv_sem)
    left = pltpu.make_async_copy(blocks, blocks, send_sem)

    if n_groups == 1:
        for i in mixed:
            outgoing(i).start()
    else:
        each(everyone - 1, lambda i: outgoing(i).start())

    for load in loads[2:]:
        load.wait()
    first = own * share

    def picked(values, at):
        lane = lax.broadcasted_iota(jnp.int32, values.shape, 1)
        return jnp.sum(jnp.where(lane == at, values, 0).astype(F32), axis=1, keepdims=True)

    row_at = lax.broadcasted_iota(jnp.int32, (width, LANES), 0)
    col_at = lax.broadcasted_iota(jnp.int32, (width, LANES), 1)
    apart = row_at - col_at
    floor_rows = []
    for k in range(share):
        win = picked(wins[...], first + k)
        floor_rows.append(jnp.broadcast_to(1e-05 * win, (1, LANES)))
        band = jnp.logical_and(apart >= 0, apart < win.astype(jnp.int32))
        bt[:, pl.ds(k * LANES, LANES)] = jnp.where(band, 1.0, 0.0).astype(BF16)
    floor_row = jnp.concatenate(floor_rows, axis=1)

    lane_at = lax.broadcasted_iota(jnp.int32, (share * GROUP, LANES), 1)

    def prepare(group):
        base = group * GROUP
        rows = lags[pl.ds(base, GROUP), :]
        lag = jnp.concatenate([picked(rows, first + k) for k in range(share)], axis=0)
        lag = jnp.broadcast_to(lag.astype(jnp.int32), (share * GROUP, LANES))
        square = (GROUP, subnet.shape[1])
        here = lax.broadcasted_iota(jnp.int32, square, 1) == base + lax.broadcasted_iota(
            jnp.int32, square, 0
        )

        def column(row):
            spread_row = jnp.broadcast_to(row.astype(F32), square)
            return jnp.sum(jnp.where(here, spread_row, 0.0), axis=1, keepdims=True)

        region = jnp.broadcast_to(column(subnet[...]).astype(jnp.int32), (GROUP, LANES))
        open_ = [column(mask[pl.ds(c, 1), :]) for c in range(CHANNELS)]
        live = jnp.maximum(functools.reduce(jnp.add, open_), 1.0)
        return lag, region, [o / live for o in open_]

    ready = prepare(0) if n_groups == 1 else None

    mirror = lax.broadcasted_iota(jnp.int32, (width, width), 0) + lax.broadcasted_iota(
        jnp.int32, (width, width), 1
    )
    mirror = jnp.where(mirror == span - 1, 1.0, 0.0).astype(BF16)
    k_dev = templates.shape[1]
    for c in range(CHANNELS):
        tpad[c, :, pl.ds(0, span)] = templates[c].astype(F32)
    mirrored = jnp.dot(
        jnp.concatenate([tpad[c] for c in range(CHANNELS)], axis=0).astype(BF16),
        mirror,
        preferred_element_type=F32,
    )
    norm_rows = []
    for c in range(CHANNELS):
        norms = []
        for k in range(share):
            taps = tpad[c, pl.ds(a_me * share + k, 1), :]
            power = jnp.sum(taps * taps, axis=1, keepdims=True)
            norms.append(jnp.broadcast_to(1.0 / jnp.sqrt(power + 1e-06), (1, LANES)))
        norm_rows.append(jnp.concatenate(norms, axis=1))
        for j in range(k_blocks):
            turned = pltpu.roll(
                mirrored[c * k_dev : (c + 1) * k_dev], (j * LANES - span + 1) % width, 1
            )
            lines[c, j] = jnp.concatenate([turned[:, :LANES], turned[:, width - LANES :]], axis=1)
            for k in range(share):
                line = lines[c, j, pl.ds(a_me * share + k, 1), :]
                slid = pltpu.roll(
                    jnp.broadcast_to(line, (LANES, 2 * LANES)), 0, 1, stride=1, stride_axis=0
                )
                wt[c, pl.ds(j * LANES, LANES), pl.ds(k * LANES, LANES)] = slid[:, :LANES].astype(BF16)

    def work(group, ready):
        lag, region, weight = ready
        for o in range(owners):
            for half in range(2):
                for c in range(CHANNELS):
                    block = recv[(group * owners + o) * 2 + half, c].astype(F32)
                    for n in range(own_blocks):
                        ebuf[c, half * own_blocks + n, pl.ds(o * st_dev, st_dev), :] = block[
                            :, n * LANES : (n + 1) * LANES
                        ]

        def spread(parts):
            empty = jnp.zeros_like(parts[0])
            parts = parts + [empty] * (u_blocks + k_blocks - 1 - len(parts))
            return jnp.concatenate(
                [jnp.concatenate(parts[j : j + u_blocks], axis=0) for j in range(k_blocks)], axis=1
            )

        waves = []
        squares = []
        for c in range(CHANNELS):
            wave = [ebuf[c, n] for n in range(2 * own_blocks)]
            waves.append(spread([w.astype(BF16) for w in wave]))
            high = [(w * w).astype(BF16) for w in wave]
            low = [(w * w - h.astype(F32)).astype(BF16) for w, h in zip(wave, high)]
            squares.append(spread(high))
            squares.append(spread(low))
        squares = jnp.concatenate(squares, axis=0)
        tall = u_blocks * GROUP
        scales = [jnp.concatenate([weight[c]] * u_blocks, axis=0) for c in range(CHANNELS)]
        for start in range(0, share, PAIR):
            count = min(PAIR, share - start)
            picks = slice(start * LANES, (start + count) * LANES)
            energy = jnp.dot(squares, bt[:, picks], preferred_element_type=F32)
            coherent = None
            for c in range(CHANNELS):
                at = 2 * c * tall
                power = energy[at : at + tall] + energy[at + tall : at + 2 * tall]
                corr = jnp.dot(waves[c], wt[c, :, picks], preferred_element_type=F32)
                scale = scales[c] * norm_rows[c][:, picks]
                term = corr * lax.rsqrt(power + floor_row[:, picks]) * scale
                coherent = term if coherent is None else coherent + term
            tops = slice(start * GROUP, (start + count) * GROUP)
            lag_pair = lag[tops]
            lanes = lane_at[tops]
            pieces = [
                jnp.concatenate(
                    [
                        coherent[b * GROUP : (b + 1) * GROUP, k * LANES : (k + 1) * LANES]
                        for k in range(count)
                    ],
                    axis=0,
                )
                for b in range(u_blocks)
            ]
            for bit in range(lag_bits):
                step = 1 << bit
                turned = [pltpu.roll(p, LANES - step, 1) for p in pieces]
                stays = lanes < LANES - step
                taken = (lax.shift_right_logical(lag_pair, bit) & 1) == 1
                pieces = [
                    jnp.where(
                        taken,
                        jnp.where(stays, turned[b], turned[min(b + 1, u_blocks - 1)]),
                        pieces[b],
                    )
                    for b in range(u_blocks)
                ]
            for k in range(count):
                for r in range(REGIONS):
                    member = region == r
                    total = jnp.concatenate(
                        [
                            jnp.sum(
                                jnp.where(member, pieces[n][k * GROUP : (k + 1) * GROUP], 0.0),
                                axis=0,
                                keepdims=True,
                            )
                            for n in range(own_blocks)
                        ],
                        axis=1,
                    )
                    if n_groups == 1:
                        out[start + k, pl.ds(r, 1), :] = total
                    else:
                        acc[start + k, pl.ds(r, 1), :] += total

    if n_groups == 1:
        arrived.wait()
        work(0, ready)
    else:
        acc[...] = jnp.zeros_like(acc)
        arrived.wait()

        def one(group, carry):
            work(group, prepare(group))
            return carry

        lax.fori_loop(0, n_groups, one, 0)
        out[...] = acc[...]
    left.wait()


def shards(traces, trace_tail, templates, win_lengths, moveouts, chan_mask, subnet):
    n_tmpl = lax.axis_size("tmpl")
    n_sta = lax.axis_size("sta")
    n_own = n_tmpl * n_sta
    st_dev, _, t_dev = traces.shape
    share = templates.shape[0] // n_sta
    span = templates.shape[2]
    width = ceil_div(LANES + span - 1, LANES) * LANES
    block = (CHANNELS, st_dev, t_dev)
    operands = (
        jnp.transpose(traces, (1, 0, 2)),
        jnp.transpose(trace_tail, (1, 0, 2)),
        jnp.transpose(templates, (1, 0, 2)),
        win_lengths.reshape(1, -1),
        moveouts.T,
        chan_mask.T,
        subnet.reshape(1, -1),
    )
    return pl.pallas_call(
        functools.partial(kernel, n_sta, n_own, share),
        out_shape=jax.ShapeDtypeStruct((share, REGIONS, t_dev), F32),
        in_specs=[pl.BlockSpec(memory_space=pltpu.HBM)] * len(operands),
        out_specs=pl.BlockSpec(memory_space=pltpu.VMEM),
        scratch_shapes=[pltpu.VMEM(x.shape, x.dtype) for x in operands[1:]]
        + [
            pltpu.VMEM(block, F32),
            pltpu.VMEM((2,) + block, BF16),
            pltpu.VMEM((2 * n_own,) + block, BF16),
            pltpu.VMEM((CHANNELS, 2 * t_dev // LANES, GROUP, LANES), F32),
            pltpu.VMEM((CHANNELS, templates.shape[0], width), F32),
            pltpu.VMEM((CHANNELS, width // LANES, templates.shape[0], 2 * LANES), F32),
            pltpu.VMEM((CHANNELS, width, share * LANES), BF16),
            pltpu.VMEM((width, share * LANES), BF16),
            pltpu.VMEM((share, REGIONS, t_dev), F32),
            pltpu.SemaphoreType.DMA((len(operands),)),
            pltpu.SemaphoreType.DMA,
            pltpu.SemaphoreType.DMA,
        ],
        compiler_params=pltpu.CompilerParams(
            collective_id=0, has_side_effects=True, vmem_limit_bytes=32 * 1024 * 1024
        ),
        name="matched_filter",
    )(*(pltpu.with_memory_space_constraint(x, pltpu.HBM) for x in operands))


def solution(mesh):
    in_specs = (
        P(("tmpl", "sta"), None, ("parts", "sub")),
        P(("tmpl", "sta"), None, "parts"),
        P("tmpl", None, None),
        P(),
        P(),
        P("parts", None),
        P(),
    )
    out_specs = P(("tmpl", "sta"), None, ("parts", "sub"))
    return jax.shard_map(shards, mesh=mesh, in_specs=in_specs, out_specs=out_specs, check_vma=False)
```

```python
import functools

import jax
import jax.numpy as jnp
from jax import lax
from jax.experimental import pallas as pl
from jax.experimental.pallas import tpu as pltpu
from jax.sharding import PartitionSpec as P

REGIONS = 2
CHANNELS = 3
LANES = 128
GROUP = 16
PAIR = 2
F32 = jnp.float32
BF16 = jnp.bfloat16


def ceil_div(a, b):
    return -(-a // b)


def each(count, body):
    if count <= 16:
        for i in range(count):
            body(i)
    else:
        lax.fori_loop(0, count, lambda i, c: (body(i), c)[1], 0)


def kernel(
    n_sta, n_own, share,
    traces_hbm, tail_hbm, templates_hbm, wins_hbm, lags_hbm, mask_hbm, subnet_hbm,
    out,
    traces, tail, templates, wins, lags, mask, subnet,
    stage, send, recv, whole, tpad, lines, wt, bt, acc, load_sem, send_sem, recv_sem,
):
    _, st_dev, t_dev = traces_hbm.shape
    halo = tail.shape[2]
    span = templates.shape[2]
    lag_bits = (halo - span).bit_length()
    own_blocks = t_dev // LANES
    u_blocks = ceil_div(t_dev + halo - span + 1, LANES)
    k_blocks = ceil_div(LANES + span - 1, LANES)
    width = k_blocks * LANES
    owners = GROUP // st_dev
    n_groups = n_own // owners
    everyone = 2 * n_own

    t_me = lax.axis_index("tmpl")
    a_me = lax.axis_index("sta")
    u_me = lax.axis_index("sub")
    own = t_me * n_sta + a_me

    def place(d):
        if isinstance(d, int):
            d_t, d_a, d_u = d // (2 * n_sta), d // 2 % n_sta, d % 2
        else:
            d_t, d_a, d_u = lax.div(d, 2 * n_sta), lax.rem(lax.div(d, 2), n_sta), lax.rem(d, 2)
        return {
            "tmpl": lax.rem(t_me + d_t, n_own // n_sta),
            "sta": lax.rem(a_me + d_a, n_sta),
            "sub": lax.rem(u_me + d_u, 2),
        }

    pairs = [
        (traces_hbm, traces), (tail_hbm, tail), (templates_hbm, templates), (wins_hbm, wins),
        (lags_hbm, lags), (mask_hbm, mask), (subnet_hbm, subnet),
    ]
    loads = [pltpu.make_async_copy(a, b, load_sem.at[i]) for i, (a, b) in enumerate(pairs)]
    barrier = pltpu.get_barrier_semaphore()

    def greet(i):
        pl.semaphore_signal(barrier, inc=1, device_id=place(i + 1), device_id_type=pl.DeviceIdType.MESH)

    order = sorted(range(everyone - 1), key=lambda i: abs(i + 1 - n_own))
    if n_groups == 1:
        for i in order:
            greet(i)
    else:
        each(everyone - 1, greet)
    for load in loads:
        load.start()

    stage[...] = jnp.zeros_like(stage)
    tpad[...] = jnp.zeros_like(tpad)
    loads[0].wait()
    loads[1].wait()
    for c in range(CHANNELS):
        stage[c, :, pl.ds(0, halo)] = tail[c].astype(F32)
        for n in range(own_blocks):
            lanes = pl.ds(n * LANES, LANES)
            main = traces[c, :, lanes]
            send[0, n, c] = main
            send[1, n, c] = jnp.where(u_me == 1, main.astype(F32), stage[c, :, lanes]).astype(BF16)
    pltpu.make_async_copy(send.at[0], recv.at[pl.ds(0, own_blocks), :, own], recv_sem).start()

    pl.semaphore_wait(barrier, everyone - 1)

    def outgoing(i):
        d = i + 1
        half = d % 2
        return pltpu.make_async_remote_copy(
            src_ref=send.at[half],
            dst_ref=recv.at[pl.ds(half * own_blocks, own_blocks), :, own],
            send_sem=send_sem,
            recv_sem=recv_sem,
            device_id=place(d),
            device_id_type=pl.DeviceIdType.MESH,
        )

    arrived = pltpu.make_async_copy(recv, recv, recv_sem)
    left = pltpu.make_async_copy(whole, whole, send_sem)

    if n_groups == 1:
        for i in order:
            outgoing(i).start()
    else:
        each(everyone - 1, lambda i: outgoing(i).start())

    for load in loads[2:]:
        load.wait()
    first = own * share

    def picked(values, at):
        lane = lax.broadcasted_iota(jnp.int32, values.shape, 1)
        return jnp.sum(jnp.where(lane == at, values, 0).astype(F32), axis=1, keepdims=True)

    row_at = lax.broadcasted_iota(jnp.int32, (width, LANES), 0)
    col_at = lax.broadcasted_iota(jnp.int32, (width, LANES), 1)
    apart = row_at - col_at
    floor_rows = []
    for k in range(share):
        win = picked(wins[...], first + k)
        floor_rows.append(jnp.broadcast_to(1e-05 * win, (1, LANES)))
        band = jnp.logical_and(apart >= 0, apart < win.astype(jnp.int32))
        bt[:, pl.ds(k * LANES, LANES)] = jnp.where(band, 1.0, 0.0).astype(BF16)
    floor_row = jnp.concatenate(floor_rows, axis=1)

    lane_at = lax.broadcasted_iota(jnp.int32, (share * GROUP, LANES), 1)

    def prepare(group):
        base = group * GROUP
        rows = lags[pl.ds(base, GROUP), :]
        lag = jnp.concatenate([picked(rows, first + k) for k in range(share)], axis=0)
        lag = jnp.broadcast_to(lag.astype(jnp.int32), (share * GROUP, LANES))
        square = (GROUP, subnet.shape[1])
        here = lax.broadcasted_iota(jnp.int32, square, 1) == base + lax.broadcasted_iota(
            jnp.int32, square, 0
        )

        def column(row):
            spread_row = jnp.broadcast_to(row.astype(F32), square)
            return jnp.sum(jnp.where(here, spread_row, 0.0), axis=1, keepdims=True)

        region = jnp.broadcast_to(column(subnet[...]).astype(jnp.int32), (GROUP, LANES))
        open_ = [column(mask[pl.ds(c, 1), :]) for c in range(CHANNELS)]
        live = jnp.maximum(functools.reduce(jnp.add, open_), 1.0)
        return lag, region, [o / live for o in open_]

    ready = prepare(0) if n_groups == 1 else None

    mirror = lax.broadcasted_iota(jnp.int32, (width, width), 0) + lax.broadcasted_iota(
        jnp.int32, (width, width), 1
    )
    mirror = jnp.where(mirror == span - 1, 1.0, 0.0).astype(BF16)
    k_dev = templates.shape[1]
    for c in range(CHANNELS):
        tpad[c, :, pl.ds(0, span)] = templates[c].astype(F32)
    mirrored = jnp.dot(
        jnp.concatenate([tpad[c] for c in range(CHANNELS)], axis=0).astype(BF16),
        mirror,
        preferred_element_type=F32,
    )
    norm_rows = []
    for c in range(CHANNELS):
        norms = []
        for k in range(share):
            taps = tpad[c, pl.ds(a_me * share + k, 1), :]
            power = jnp.sum(taps * taps, axis=1, keepdims=True)
            norms.append(jnp.broadcast_to(1.0 / jnp.sqrt(power + 1e-06), (1, LANES)))
        norm_rows.append(jnp.concatenate(norms, axis=1))
        for j in range(k_blocks):
            turned = pltpu.roll(
                mirrored[c * k_dev : (c + 1) * k_dev], (j * LANES - span + 1) % width, 1
            )
            lines[c, j] = jnp.concatenate([turned[:, :LANES], turned[:, width - LANES :]], axis=1)
            for k in range(share):
                line = lines[c, j, pl.ds(a_me * share + k, 1), :]
                slid = pltpu.roll(
                    jnp.broadcast_to(line, (LANES, 2 * LANES)), 0, 1, stride=1, stride_axis=0
                )
                wt[c, pl.ds(j * LANES, LANES), pl.ds(k * LANES, LANES)] = slid[:, :LANES].astype(BF16)

    def work(group, ready):
        lag, region, weight = ready
        stations = recv.reshape(2 * own_blocks, CHANNELS, n_own * st_dev, LANES)
        rows = pl.ds(group * GROUP, GROUP)

        def spread(parts):
            empty = jnp.zeros_like(parts[0])
            parts = parts + [empty] * (u_blocks + k_blocks - 1 - len(parts))
            return jnp.concatenate(
                [jnp.concatenate(parts[j : j + u_blocks], axis=0) for j in range(k_blocks)], axis=1
            )

        waves = []
        squares = []
        for c in range(CHANNELS):
            wave = [stations[n, c, rows, :] for n in range(2 * own_blocks)]
            waves.append(spread(wave))
            wave = [w.astype(F32) for w in wave]
            high = [(w * w).astype(BF16) for w in wave]
            low = [(w * w - h.astype(F32)).astype(BF16) for w, h in zip(wave, high)]
            squares.append(spread(high))
            squares.append(spread(low))
        squares = jnp.concatenate(squares, axis=0)
        tall = u_blocks * GROUP
        scales = [jnp.concatenate([weight[c]] * u_blocks, axis=0) for c in range(CHANNELS)]
        for start in range(0, share, PAIR):
            count = min(PAIR, share - start)
            picks = slice(start * LANES, (start + count) * LANES)
            energy = jnp.dot(squares, bt[:, picks], preferred_element_type=F32)
            coherent = None
            for c in range(CHANNELS):
                at = 2 * c * tall
                power = energy[at : at + tall] + energy[at + tall : at + 2 * tall]
                corr = jnp.dot(waves[c], wt[c, :, picks], preferred_element_type=F32)
                scale = scales[c] * norm_rows[c][:, picks]
                term = corr * lax.rsqrt(power + floor_row[:, picks]) * scale
                coherent = term if coherent is None else coherent + term
            tops = slice(start * GROUP, (start + count) * GROUP)
            lag_pair = lag[tops]
            lanes = lane_at[tops]
            pieces = [
                jnp.concatenate(
                    [
                        coherent[b * GROUP : (b + 1) * GROUP, k * LANES : (k + 1) * LANES]
                        for k in range(count)
                    ],
                    axis=0,
                )
                for b in range(u_blocks)
            ]
            for bit in range(lag_bits):
                step = 1 << bit
                turned = [pltpu.roll(p, LANES - step, 1) for p in pieces]
                stays = lanes < LANES - step
                taken = (lax.shift_right_logical(lag_pair, bit) & 1) == 1
                pieces = [
                    jnp.where(
                        taken,
                        jnp.where(stays, turned[b], turned[min(b + 1, u_blocks - 1)]),
                        pieces[b],
                    )
                    for b in range(u_blocks)
                ]
            for k in range(count):
                for r in range(REGIONS):
                    member = region == r
                    total = jnp.concatenate(
                        [
                            jnp.sum(
                                jnp.where(member, pieces[n][k * GROUP : (k + 1) * GROUP], 0.0),
                                axis=0,
                                keepdims=True,
                            )
                            for n in range(own_blocks)
                        ],
                        axis=1,
                    )
                    if n_groups == 1:
                        out[start + k, pl.ds(r, 1), :] = total
                    else:
                        acc[start + k, pl.ds(r, 1), :] += total

    if n_groups == 1:
        arrived.wait()
        work(0, ready)
    else:
        acc[...] = jnp.zeros_like(acc)
        arrived.wait()

        def one(group, carry):
            work(group, prepare(group))
            return carry

        lax.fori_loop(0, n_groups, one, 0)
        out[...] = acc[...]
    left.wait()


def shards(traces, trace_tail, templates, win_lengths, moveouts, chan_mask, subnet):
    n_tmpl = lax.axis_size("tmpl")
    n_sta = lax.axis_size("sta")
    n_own = n_tmpl * n_sta
    st_dev, _, t_dev = traces.shape
    share = templates.shape[0] // n_sta
    span = templates.shape[2]
    width = ceil_div(LANES + span - 1, LANES) * LANES
    blocks = t_dev // LANES
    operands = (
        jnp.transpose(traces, (1, 0, 2)),
        jnp.transpose(trace_tail, (1, 0, 2)),
        jnp.transpose(templates, (1, 0, 2)),
        win_lengths.reshape(1, -1),
        moveouts.T,
        chan_mask.T,
        subnet.reshape(1, -1),
    )
    return pl.pallas_call(
        functools.partial(kernel, n_sta, n_own, share),
        out_shape=jax.ShapeDtypeStruct((share, REGIONS, t_dev), F32),
        in_specs=[pl.BlockSpec(memory_space=pltpu.HBM)] * len(operands),
        out_specs=pl.BlockSpec(memory_space=pltpu.VMEM),
        scratch_shapes=[pltpu.VMEM(x.shape, x.dtype) for x in operands]
        + [
            pltpu.VMEM((CHANNELS, st_dev, t_dev), F32),
            pltpu.VMEM((2, blocks, CHANNELS, st_dev, LANES), BF16),
            pltpu.VMEM((2 * blocks, CHANNELS, n_own, st_dev, LANES), BF16),
            pltpu.VMEM((2 * n_own - 1, blocks, CHANNELS, st_dev, LANES), BF16),
            pltpu.VMEM((CHANNELS, templates.shape[0], width), F32),
            pltpu.VMEM((CHANNELS, width // LANES, templates.shape[0], 2 * LANES), F32),
            pltpu.VMEM((CHANNELS, width, share * LANES), BF16),
            pltpu.VMEM((width, share * LANES), BF16),
            pltpu.VMEM((share, REGIONS, t_dev), F32),
            pltpu.SemaphoreType.DMA((len(operands),)),
            pltpu.SemaphoreType.DMA,
            pltpu.SemaphoreType.DMA,
        ],
        compiler_params=pltpu.CompilerParams(
            collective_id=0, has_side_effects=True, vmem_limit_bytes=32 * 1024 * 1024
        ),
        name="matched_filter",
    )(*(pltpu.with_memory_space_constraint(x, pltpu.HBM) for x in operands))


def solution(mesh):
    in_specs = (
        P(("tmpl", "sta"), None, ("parts", "sub")),
        P(("tmpl", "sta"), None, "parts"),
        P("tmpl", None, None),
        P(),
        P(),
        P("parts", None),
        P(),
    )
    out_specs = P(("tmpl", "sta"), None, ("parts", "sub"))
    return jax.shard_map(shards, mesh=mesh, in_specs=in_specs, out_specs=out_specs, check_vma=False)
```

```python
import functools

import jax
import jax.numpy as jnp
from jax import lax
from jax.experimental import pallas as pl
from jax.experimental.pallas import tpu as pltpu
from jax.sharding import PartitionSpec as P

REGIONS = 2
CHANNELS = 3
LANES = 128
GROUP = 16
PAIR = 2
F32 = jnp.float32
BF16 = jnp.bfloat16


def ceil_div(a, b):
    return -(-a // b)


def each(count, body):
    if count <= 16:
        for i in range(count):
            body(i)
    else:
        lax.fori_loop(0, count, lambda i, c: (body(i), c)[1], 0)


def kernel(
    n_sta, n_own, share,
    traces_hbm, tail_hbm, templates_hbm, wins_hbm, lags_hbm, mask_hbm, subnet_hbm,
    out,
    traces, tail, templates, wins, lags, mask, subnet,
    stage, send, recv, whole, tpad, lines, wt, bt, acc, load_sem, send_sem, recv_sem,
):
    _, st_dev, t_dev = traces_hbm.shape
    halo = tail.shape[2]
    span = templates.shape[2]
    lag_bits = (halo - span).bit_length()
    own_blocks = t_dev // LANES
    u_blocks = ceil_div(t_dev + halo - span + 1, LANES)
    k_blocks = ceil_div(LANES + span - 1, LANES)
    width = k_blocks * LANES
    owners = GROUP // st_dev
    n_groups = n_own // owners
    everyone = 2 * n_own

    t_me = lax.axis_index("tmpl")
    a_me = lax.axis_index("sta")
    u_me = lax.axis_index("sub")
    own = t_me * n_sta + a_me

    def place(d):
        if isinstance(d, int):
            d_t, d_a, d_u = d // (2 * n_sta), d // 2 % n_sta, d % 2
        else:
            d_t, d_a, d_u = lax.div(d, 2 * n_sta), lax.rem(lax.div(d, 2), n_sta), lax.rem(d, 2)
        return {
            "tmpl": lax.rem(t_me + d_t, n_own // n_sta),
            "sta": lax.rem(a_me + d_a, n_sta),
            "sub": lax.rem(u_me + d_u, 2),
        }

    pairs = [
        (traces_hbm, traces), (tail_hbm, tail), (templates_hbm, templates), (wins_hbm, wins),
        (lags_hbm, lags), (mask_hbm, mask), (subnet_hbm, subnet),
    ]
    loads = [pltpu.make_async_copy(a, b, load_sem.at[i]) for i, (a, b) in enumerate(pairs)]
    barrier = pltpu.get_barrier_semaphore()

    def greet(i):
        pl.semaphore_signal(barrier, inc=1, device_id=place(i + 1), device_id_type=pl.DeviceIdType.MESH)

    order = sorted(range(everyone - 1), key=lambda i: abs(i + 1 - n_own))
    if n_groups == 1:
        for i in order:
            greet(i)
    else:
        each(everyone - 1, greet)
    for load in loads:
        load.start()

    stage[...] = jnp.zeros_like(stage)
    tpad[...] = jnp.zeros_like(tpad)
    loads[0].wait()
    loads[1].wait()
    for c in range(CHANNELS):
        stage[c, :, pl.ds(0, halo)] = tail[c].astype(F32)
        for n in range(own_blocks):
            lanes = pl.ds(n * LANES, LANES)
            main = traces[c, :, lanes]
            send[0, n, c] = main
            send[1, n, c] = jnp.where(u_me == 1, main.astype(F32), stage[c, :, lanes]).astype(BF16)
    pltpu.make_async_copy(send.at[0], recv.at[pl.ds(0, own_blocks), :, own], recv_sem).start()

    pl.semaphore_wait(barrier, everyone - 1)

    def outgoing(i):
        d = i + 1
        half = d % 2
        return pltpu.make_async_remote_copy(
            src_ref=send.at[half],
            dst_ref=recv.at[pl.ds(half * own_blocks, own_blocks), :, own],
            send_sem=send_sem,
            recv_sem=recv_sem,
            device_id=place(d),
            device_id_type=pl.DeviceIdType.MESH,
        )

    arrived = pltpu.make_async_copy(recv, recv, recv_sem)
    left = pltpu.make_async_copy(whole, whole, send_sem)

    if n_groups == 1:
        for i in order:
            outgoing(i).start()
    else:
        each(everyone - 1, lambda i: outgoing(i).start())

    for load in loads[2:]:
        load.wait()
    first = own * share

    def picked(values, at):
        lane = lax.broadcasted_iota(jnp.int32, values.shape, 1)
        return jnp.sum(jnp.where(lane == at, values, 0).astype(F32), axis=1, keepdims=True)

    row_at = lax.broadcasted_iota(jnp.int32, (width, LANES), 0)
    col_at = lax.broadcasted_iota(jnp.int32, (width, LANES), 1)
    apart = row_at - col_at
    floor_rows = []
    for k in range(share):
        win = picked(wins[...], first + k)
        floor_rows.append(jnp.broadcast_to(1e-05 * win, (1, LANES)))
        band = jnp.logical_and(apart >= 0, apart < win.astype(jnp.int32))
        bt[:, pl.ds(k * LANES, LANES)] = jnp.where(band, 1.0, 0.0).astype(BF16)
    floor_row = jnp.concatenate(floor_rows, axis=1)

    lane_at = lax.broadcasted_iota(jnp.int32, (share * GROUP, LANES), 1)

    def prepare(group):
        base = group * GROUP
        rows = lags[pl.ds(base, GROUP), :]
        lag = jnp.concatenate([picked(rows, first + k) for k in range(share)], axis=0)
        lag = jnp.broadcast_to(lag.astype(jnp.int32), (share * GROUP, LANES))
        square = (GROUP, subnet.shape[1])
        here = lax.broadcasted_iota(jnp.int32, square, 1) == base + lax.broadcasted_iota(
            jnp.int32, square, 0
        )

        def column(row):
            spread_row = jnp.broadcast_to(row.astype(F32), square)
            return jnp.sum(jnp.where(here, spread_row, 0.0), axis=1, keepdims=True)

        region = jnp.broadcast_to(column(subnet[...]).astype(jnp.int32), (GROUP, LANES))
        open_ = [column(mask[pl.ds(c, 1), :]) for c in range(CHANNELS)]
        live = jnp.maximum(functools.reduce(jnp.add, open_), 1.0)
        return lag, region, [o / live for o in open_]

    ready = prepare(0) if n_groups == 1 else None

    mirror = lax.broadcasted_iota(jnp.int32, (width, width), 0) + lax.broadcasted_iota(
        jnp.int32, (width, width), 1
    )
    mirror = jnp.where(mirror == span - 1, 1.0, 0.0).astype(BF16)
    k_dev = templates.shape[1]
    for c in range(CHANNELS):
        tpad[c, :, pl.ds(0, span)] = templates[c].astype(F32)
    mirrored = jnp.dot(
        jnp.concatenate([tpad[c] for c in range(CHANNELS)], axis=0).astype(BF16),
        mirror,
        preferred_element_type=F32,
    )
    norm_rows = []
    for c in range(CHANNELS):
        norms = []
        for k in range(share):
            taps = tpad[c, pl.ds(a_me * share + k, 1), :]
            power = jnp.sum(taps * taps, axis=1, keepdims=True)
            norms.append(jnp.broadcast_to(1.0 / jnp.sqrt(power + 1e-06), (1, LANES)))
        norm_rows.append(jnp.concatenate(norms, axis=1))
        for j in range(k_blocks):
            turned = pltpu.roll(
                mirrored[c * k_dev : (c + 1) * k_dev], (j * LANES - span + 1) % width, 1
            )
            lines[c, j] = jnp.concatenate([turned[:, :LANES], turned[:, width - LANES :]], axis=1)
            for k in range(share):
                line = lines[c, j, pl.ds(a_me * share + k, 1), :]
                slid = pltpu.roll(
                    jnp.broadcast_to(line, (LANES, 2 * LANES)), 0, 1, stride=1, stride_axis=0
                )
                wt[c, pl.ds(j * LANES, LANES), pl.ds(k * LANES, LANES)] = slid[:, :LANES].astype(BF16)

    def work(group, ready):
        lag, region, weight = ready
        stations = recv.reshape(2 * own_blocks, CHANNELS, n_own * st_dev, LANES)
        rows = pl.ds(group * GROUP, GROUP)

        def spread(parts):
            empty = jnp.zeros_like(parts[0])
            parts = parts + [empty] * (u_blocks + k_blocks - 1 - len(parts))
            return jnp.concatenate(
                [jnp.concatenate(parts[j : j + u_blocks], axis=0) for j in range(k_blocks)], axis=1
            )

        waves = []
        squares = []
        for c in range(CHANNELS):
            wave = [stations[n, c, rows, :] for n in range(2 * own_blocks)]
            waves.append(spread(wave))
            wave = [w.astype(F32) for w in wave]
            high = [(w * w).astype(BF16) for w in wave]
            low = [(w * w - h.astype(F32)).astype(BF16) for w, h in zip(wave, high)]
            squares.append(spread(high))
            squares.append(spread(low))
        squares = jnp.concatenate(squares, axis=0)
        tall = u_blocks * GROUP
        scales = [jnp.concatenate([weight[c]] * u_blocks, axis=0) for c in range(CHANNELS)]
        for start in range(0, share, PAIR):
            count = min(PAIR, share - start)
            picks = slice(start * LANES, (start + count) * LANES)
            energy = jnp.dot(squares, bt[:, picks], preferred_element_type=F32)
            coherent = None
            for c in range(CHANNELS):
                at = 2 * c * tall
                power = energy[at : at + tall] + energy[at + tall : at + 2 * tall]
                corr = jnp.dot(waves[c], wt[c, :, picks], preferred_element_type=F32)
                scale = scales[c] * norm_rows[c][:, picks]
                term = corr * lax.rsqrt(power + floor_row[:, picks]) * scale
                coherent = term if coherent is None else coherent + term
            tops = slice(start * GROUP, (start + count) * GROUP)
            lag_pair = lag[tops]
            lanes = lane_at[tops]
            pieces = [
                jnp.concatenate(
                    [
                        coherent[b * GROUP : (b + 1) * GROUP, k * LANES : (k + 1) * LANES]
                        for k in range(count)
                    ],
                    axis=0,
                )
                for b in range(u_blocks)
            ]
            for bit in range(lag_bits):
                step = 1 << bit
                turned = [pltpu.roll(p, LANES - step, 1) for p in pieces]
                stays = lanes < LANES - step
                taken = (lax.shift_right_logical(lag_pair, bit) & 1) == 1
                pieces = [
                    jnp.where(
                        taken,
                        jnp.where(stays, turned[b], turned[min(b + 1, u_blocks - 1)]),
                        pieces[b],
                    )
                    for b in range(u_blocks)
                ]
            for k in range(count):
                for r in range(REGIONS):
                    member = region == r
                    total = jnp.concatenate(
                        [
                            jnp.sum(
                                jnp.where(member, pieces[n][k * GROUP : (k + 1) * GROUP], 0.0),
                                axis=0,
                                keepdims=True,
                            )
                            for n in range(own_blocks)
                        ],
                        axis=1,
                    )
                    if n_groups == 1:
                        out[start + k, pl.ds(r, 1), :] = total
                    else:
                        acc[start + k, pl.ds(r, 1), :] += total

    left.wait()
    if n_groups == 1:
        arrived.wait()
        work(0, ready)
    else:
        acc[...] = jnp.zeros_like(acc)
        arrived.wait()

        def one(group, carry):
            work(group, prepare(group))
            return carry

        lax.fori_loop(0, n_groups, one, 0)
        out[...] = acc[...]


def shards(traces, trace_tail, templates, win_lengths, moveouts, chan_mask, subnet):
    n_tmpl = lax.axis_size("tmpl")
    n_sta = lax.axis_size("sta")
    n_own = n_tmpl * n_sta
    st_dev, _, t_dev = traces.shape
    share = templates.shape[0] // n_sta
    span = templates.shape[2]
    width = ceil_div(LANES + span - 1, LANES) * LANES
    blocks = t_dev // LANES
    operands = (
        jnp.transpose(traces, (1, 0, 2)),
        jnp.transpose(trace_tail, (1, 0, 2)),
        jnp.transpose(templates, (1, 0, 2)),
        win_lengths.reshape(1, -1),
        moveouts.T,
        chan_mask.T,
        subnet.reshape(1, -1),
    )
    return pl.pallas_call(
        functools.partial(kernel, n_sta, n_own, share),
        out_shape=jax.ShapeDtypeStruct((share, REGIONS, t_dev), F32),
        in_specs=[pl.BlockSpec(memory_space=pltpu.HBM)] * len(operands),
        out_specs=pl.BlockSpec(memory_space=pltpu.VMEM),
        scratch_shapes=[pltpu.VMEM(x.shape, x.dtype) for x in operands]
        + [
            pltpu.VMEM((CHANNELS, st_dev, t_dev), F32),
            pltpu.VMEM((2, blocks, CHANNELS, st_dev, LANES), BF16),
            pltpu.VMEM((2 * blocks, CHANNELS, n_own, st_dev, LANES), BF16),
            pltpu.VMEM((2 * n_own - 1, blocks, CHANNELS, st_dev, LANES), BF16),
            pltpu.VMEM((CHANNELS, templates.shape[0], width), F32),
            pltpu.VMEM((CHANNELS, width // LANES, templates.shape[0], 2 * LANES), F32),
            pltpu.VMEM((CHANNELS, width, share * LANES), BF16),
            pltpu.VMEM((width, share * LANES), BF16),
            pltpu.VMEM((share, REGIONS, t_dev), F32),
            pltpu.SemaphoreType.DMA((len(operands),)),
            pltpu.SemaphoreType.DMA,
            pltpu.SemaphoreType.DMA,
        ],
        compiler_params=pltpu.CompilerParams(
            collective_id=0, has_side_effects=True, vmem_limit_bytes=32 * 1024 * 1024
        ),
        name="matched_filter",
    )(*(pltpu.with_memory_space_constraint(x, pltpu.HBM) for x in operands))


def solution(mesh):
    in_specs = (
        P(("tmpl", "sta"), None, ("parts", "sub")),
        P(("tmpl", "sta"), None, "parts"),
        P("tmpl", None, None),
        P(),
        P(),
        P("parts", None),
        P(),
    )
    out_specs = P(("tmpl", "sta"), None, ("parts", "sub"))
    return jax.shard_map(shards, mesh=mesh, in_specs=in_specs, out_specs=out_specs, check_vma=False)
```
